128 devices in a mesh: expert: 32 (over z, x, core), group: 4 (over y).
Axes of the slice: x: 4, y: 4, z: 4, core: 2. Of those that a mesh axis runs over, the one named last changes fastest.
Arguments:
- tokens: bfloat16 [4096, 7168], P('expert', 'group'), may hold values from -6 to 6
- routes: int32 [4096, 8], P('expert'), may hold values from 0 to 31, all different within a row; in each aligned block of 128 rows (0 to 127, 128 to 255, ...) at most 36 rows name the same one
- route_weight: float32 [4096, 8], P('expert'), may hold values from 0.1 to 0.6
- gate_weight: bfloat16 [32, 7168, 2048], P('expert', None, 'group'), may hold values from -0.0625 to 0.0625
- up_weight: bfloat16 [32, 7168, 2048], P('expert', None, 'group'), may hold values from -0.0625 to 0.0625
- down_weight: bfloat16 [32, 2048, 7168], P('expert', 'group'), may hold values from -0.125 to 0.125
- delta_values: bfloat16 [8192, 16384], P(('expert', 'group')), may hold values from -6 to 6
- delta_owner: int32 [128, 64], P(('expert', 'group')), may hold values from 0 to 127, as said below
- delta_index: int32 [128, 64], P(('expert', 'group')), may hold values from 0 to 671
- delta_scale: int32 [128, 64], P(('expert', 'group')), may hold values from -1 to 1
- delta_count: int32 [128], P(('expert', 'group')), may hold values from 40 to 64, as said below
Outputs:
- mixed: bfloat16 [4096, 7168], P('expert', 'group')
The draws below stay inside these ranges and needn't reach their ends.
Inputs may be any that keep to these rules, and one draw needn't show every extreme that they name: `routes`: in the 128 rows of one index of expert no expert is named more than 36 times. `delta_owner`: the entries of one device's list name different owners. One owner is named among the first delta_count entries of every device's list. `delta_count`: some device has all 64 entries live.
All inputs are finite; a program needn't handle non-finite values.
Results may differ from the reference program's by a relative error of at most 0.015.
Values may be sent and summed in bfloat16 or wider, within the bound.
No kernel may reach another device: no remote copies, remote signals or barrier semaphores. Data moves between devices by JAX's collectives and lax.ppermute only.
A program may use at most 320 MiB of HBM per device.

```python
import math
import jax
import jax.numpy as jnp
import numpy as np
from jax import lax

D = 7168
FF = 2048
TOPK = 8
BLOCK = 128
TOK_DEV = 128
EXPERTS = 32
TOKENS = 4096
CAP = 36
SOURCES = 128
NB_DEV = 64
BLOCKS_MAT = 224
N_EXPERT = 32
N_GROUP = 4


def delta_lists(key):
    sources = N_EXPERT * N_GROUP
    key_count, key_full, key_hot, key_place, key_orders = jax.random.split(key, 5)
    list_count = jax.random.randint(key_count, (sources,), NB_DEV * 5 // 8, NB_DEV + 1)
    full_source = jax.random.randint(key_full, (), 0, sources)
    row_ids = jnp.arange(sources)
    list_count = jnp.where(row_ids == full_source, NB_DEV, list_count)
    hot_owner = jax.random.randint(key_hot, (), 0, sources)
    hot_place = jax.random.randint(key_place, (sources,), 0, list_count)
    sub_keys = jax.random.split(key_orders, sources)
    orders = jax.vmap(lambda sub_key: jax.random.permutation(sub_key, sources))(sub_keys)
    hot_index = jnp.argmax(orders == hot_owner, axis=1)
    displaced = orders[row_ids, hot_place]
    orders = orders.at[row_ids, hot_index].set(displaced)
    orders = orders.at[row_ids, hot_place].set(hot_owner)
    return (orders[:, :NB_DEV].astype(jnp.int32), list_count.astype(jnp.int32))


def draw_delta_owner(key, part):
    owners, counts = delta_lists(key)
    return owners


def draw_delta_count(key, part):
    owners, counts = delta_lists(key)
    return counts


def place_ends(values, own_key, smallest, top_value):
    longest = values.shape.index(max(values.shape))
    spots = []
    for shift in (0, 1):
        where = [jax.random.randint(jax.random.fold_in(own_key, axis), (), 0, length) for axis, length in enumerate(values.shape)]
        where[longest] = (where[longest] + shift) % values.shape[longest]
        spots.append(tuple(where))
    return values.at[spots[0]].set(smallest).at[spots[1]].set(top_value)


def block_scale(rng, shape, cuts, smallest, high):
    loudness, own = 1.0, jax.random.fold_in(rng, 6)
    for axis_at, blocks in cuts:
        draws = jnp.exp(jax.random.uniform(jax.random.fold_in(own, axis_at), (blocks,), jnp.float32, smallest / len(cuts), high / len(cuts)))
        loudness = loudness * jnp.repeat(draws, shape[axis_at] // blocks).reshape([-1 if axis == axis_at else 1 for axis in range(len(shape))])
    return loudness


def shared_out(stream_key, own, number, rows, number_of, top, limit, lean):
    sequence = jax.random.permutation(stream_key, number_of)
    packed, usual = shares(number_of, rows * top, limit, lean, True), shares(number_of, rows * top, limit, lean, False)
    places = jnp.arange(number_of)

    def named(sizes, rotation):
        used = int((sizes > 0).sum())
        fixed = max(1, used // 4)
        passed = fixed + (places - fixed + rotation * (used - fixed)) % max(1, number_of - fixed)
        return jnp.zeros((number_of,), jnp.int32).at[sequence[jnp.where(places < fixed, places, passed)]].set(jnp.asarray(sizes, jnp.int32))

    sizes = jnp.where(number % 4 == 0, named(packed, number // 4), named(usual, number - number // 4 - 1))
    mixed = jax.random.permutation(jax.random.fold_in(own, 3), number_of)
    donor, taker = mixed[0:number_of // 2 * 2:2], mixed[1:number_of // 2 * 2:2]
    slack = jnp.minimum(sizes[donor] - 1, limit - sizes[taker]) // 2
    slack = jnp.where((donor == sequence[0]) | (taker == sequence[0]) | (sizes[taker] == 0), 0, jnp.maximum(slack, 0))
    passed = jax.random.randint(jax.random.fold_in(own, 4), (number_of // 2,), 0, 1 << 20) % (slack + 1)
    sizes = sizes.at[donor].add(-passed).at[taker].add(passed)
    members = jnp.searchsorted(jnp.cumsum(sizes), jnp.arange(rows * top), side="right").astype(jnp.int32)
    table = members.reshape(top, rows).T
    table = table[jax.random.permutation(jax.random.fold_in(own, 1), rows)]
    rotation = jax.random.randint(jax.random.fold_in(own, 2), (rows, 1), 0, top)
    return jnp.take_along_axis(table, (jnp.arange(top)[None, :] + rotation) % top, axis=1)


def shares(amount, total, reach, lean, full):
    loads = [(1 << 20) // math.isqrt(grade ** lean) + 1 for grade in range(1, amount + 1)]
    largest = reach if full else min(reach, max(-(-total // amount), total * loads[0] // sum(loads)))
    least = 1 if total - largest >= amount - 1 else 0
    given, rest = [largest] + [least] * (amount - 1), total - largest - least * (amount - 1)
    while rest > 0:
        free = [i for i in range(1, amount) if given[i] < largest] or [i for i in range(1, amount) if given[i] < reach]
        pool, remaining = sum([loads[i] for i in free]), rest
        for i in free:
            addition = min(reach - given[i], max(1, remaining * loads[i] // pool), rest)
            given[i] = given[i] + addition
            rest = rest - addition
    return np.array(given)


def gaussian(own_key, dims, deviation, most, shards=(), kind=jnp.bfloat16):
    values = deviation * jax.random.normal(own_key, dims, jnp.float32)
    if shards:
        values = values * block_scale(own_key, dims, shards, -0.22, 0.18)
    return jnp.clip(values, -most, most).astype(kind)


def setup_inputs(seed: int = 0) -> dict:
    splits = jax.random.split(jax.random.key(seed), 12)
    tokens = gaussian(splits[0], (TOKENS, D), 1.0, 6.0, ((0, 32), (1, 4)))
    routes_keys = jax.random.split(jax.random.fold_in(splits[1], 1), TOKENS // TOK_DEV)
    routes_turns = jax.random.permutation(jax.random.fold_in(splits[1], 3), TOKENS // TOK_DEV)
    routes = jax.vmap(lambda own, number: shared_out(jax.random.fold_in(splits[1], 2), own, number, TOK_DEV, EXPERTS, TOPK, CAP, 2))(routes_keys, routes_turns).reshape((TOKENS, TOPK))
    route_weight = jnp.clip(0.1 + 0.5 * jax.random.uniform(splits[2], (TOKENS, TOPK), jnp.float32) ** block_scale(splits[2], (TOKENS, TOPK), ((0, 32),), -0.2, 0.2), 0.1, 0.6)
    gate_weight = gaussian(splits[3], (EXPERTS, D, FF), D ** -0.5, 0.0625, ((0, 32), (2, 4)))
    up_weight = gaussian(splits[4], (EXPERTS, D, FF), D ** -0.5, 0.0625, ((0, 32), (2, 4)))
    down_weight = gaussian(splits[5], (EXPERTS, FF, D), FF ** -0.5, 0.125, ((0, 32), (1, 4)))
    delta_values = gaussian(splits[6], (SOURCES * NB_DEV, BLOCK * BLOCK), 1.0, 6.0, ((0, 128),))
    delta_owner = draw_delta_owner(jax.random.fold_in(splits[11], 71), 0)
    delta_index = place_ends(jax.random.randint(splits[8], (SOURCES, NB_DEV), 0, 3 * BLOCKS_MAT), jax.random.fold_in(splits[8], 1), 0, (3 * BLOCKS_MAT) - 1).astype(jnp.int32)
    delta_scale = place_ends(jax.random.randint(splits[9], (SOURCES, NB_DEV), -1, 2), jax.random.fold_in(splits[9], 1), -1, 1).astype(jnp.int32)
    delta_count = draw_delta_count(jax.random.fold_in(splits[11], 71), 0)
    return {"tokens": tokens, "routes": routes, "route_weight": route_weight, "gate_weight": gate_weight, "up_weight": up_weight, "down_weight": down_weight, "delta_values": delta_values, "delta_owner": delta_owner, "delta_index": delta_index, "delta_scale": delta_scale, "delta_count": delta_count}


def refresh_in(weight, blocks, factor):
    hidden_loc = weight.shape[1]
    grid = blocks.reshape(D // BLOCK, hidden_loc // BLOCK, BLOCK, BLOCK)
    grid = grid.transpose(0, 2, 1, 3).reshape(D, hidden_loc)
    return (weight.astype(jnp.float32) + factor * grid).astype(jnp.bfloat16)


def refresh_down(weight, blocks, factor):
    hidden_loc = weight.shape[0]
    grid = blocks.reshape(hidden_loc // BLOCK, D // BLOCK, BLOCK, BLOCK)
    grid = grid.transpose(0, 2, 1, 3).reshape(hidden_loc, D)
    return (weight.astype(jnp.float32) + factor * grid).astype(jnp.bfloat16)


def reference(tokens, routes, route_weight, gate_weight, up_weight, down_weight, delta_values, delta_owner, delta_index, delta_scale, delta_count):
    hidden_loc = FF // N_GROUP
    blocks_mat = (D // BLOCK) * (hidden_loc // BLOCK)
    per_owner = 3 * blocks_mat
    per_expert = N_GROUP * per_owner
    is_live = jnp.arange(NB_DEV, dtype=jnp.int32)[None, :] < delta_count[:, None]
    target = jnp.where(is_live, delta_owner * per_owner + delta_index, SOURCES * per_owner).reshape(-1).astype(jnp.int32)
    scaled = delta_values.astype(jnp.float32) * jnp.exp2(delta_scale.reshape(-1).astype(jnp.float32))[:, None]

    flat_rows = routes.reshape(N_EXPERT, TOK_DEV * TOPK)
    one_hot = (flat_rows[:, :, None] == jnp.arange(EXPERTS, dtype=jnp.int32)[None, None, :]).astype(jnp.int32)
    running = jnp.cumsum(one_hot, axis=1)
    slot_number = jnp.take_along_axis(running, flat_rows[:, :, None], axis=2)[:, :, 0] - 1
    source_ids = jnp.broadcast_to(jnp.arange(N_EXPERT, dtype=jnp.int32)[:, None], flat_rows.shape)
    token_ids = jnp.arange(TOKENS * TOPK, dtype=jnp.int32) // TOPK
    expert_rows = jnp.zeros((EXPERTS, CAP, N_EXPERT, D), jnp.bfloat16)
    expert_rows = expert_rows.at[flat_rows.reshape(-1), slot_number.reshape(-1), source_ids.reshape(-1)].set(tokens[token_ids])

    def one_expert(expert_id):
        local = target - expert_id * per_expert
        local = jnp.where((local >= 0) & (local < per_expert), local, per_expert).astype(jnp.int32)
        accumulated = jnp.zeros((per_expert, BLOCK * BLOCK), jnp.float32).at[local].add(scaled, mode="drop")
        accumulated = accumulated.reshape(N_GROUP, 3, blocks_mat, BLOCK, BLOCK)
        rows_in = expert_rows[expert_id].reshape(CAP * N_EXPERT, D)
        total = jnp.zeros((CAP * N_EXPERT, D), jnp.float32)
        for member in range(N_GROUP):
            columns = slice(member * hidden_loc, (member + 1) * hidden_loc)
            gate_new = refresh_in(gate_weight[expert_id][:, columns], accumulated[member, 0], D ** -0.5)
            up_new = refresh_in(up_weight[expert_id][:, columns], accumulated[member, 1], D ** -0.5)
            down_new = refresh_down(down_weight[expert_id][columns, :], accumulated[member, 2], FF ** -0.5)
            gate_act = jnp.dot(rows_in, gate_new, preferred_element_type=jnp.float32)
            up_act = jnp.dot(rows_in, up_new, preferred_element_type=jnp.float32)
            hidden = (jax.nn.silu(gate_act) * up_act).astype(jnp.bfloat16)
            partial_value = jnp.dot(hidden, down_new, preferred_element_type=jnp.float32).astype(jnp.bfloat16)
            total = total + partial_value.astype(jnp.float32)
        return total.astype(jnp.bfloat16)

    expert_out = lax.map(one_expert, jnp.arange(EXPERTS, dtype=jnp.int32))
    expert_out = expert_out.reshape(EXPERTS, CAP, N_EXPERT, D)
    picked = expert_out[flat_rows, slot_number, source_ids].reshape(TOKENS, TOPK, D)
    result = jnp.sum(route_weight[:, :, None] * picked.astype(jnp.float32), axis=1)
    return result.astype(jnp.bfloat16)
```

```python
import functools

import jax
import jax.numpy as jnp
from jax import lax
from jax.experimental import pallas as pl
from jax.experimental.pallas import tpu as pltpu
from jax.sharding import PartitionSpec as P

BLOCK = 128
META = 16
SLOTS_A = 24
SLOTS_B = 8
SLOTS_C = 4
VMEM_LIMIT = 60 * 2**20
BF16 = jnp.bfloat16
F32 = jnp.float32
LIGHT = pl.CostEstimate(flops=0, bytes_accessed=0, transcendentals=0)
HBM = pl.BlockSpec(memory_space=pltpu.HBM)


def ring(n, shift):
    return [(i, (i + shift) % n) for i in range(n)]


def spread_kernel(owner_ref, count_ref, blocks_ref, meta_ref, out_ref):
    out_ref[:, BLOCK:, :] = meta_ref[...]

    def put(i, carry):
        out_ref[owner_ref[i], :BLOCK, :] = blocks_ref[i]
        return carry

    lax.fori_loop(0, count_ref[0], put, 0)


def spread_blocks(owner, count, blocks, meta):
    sources = meta.shape[0]
    shape = (sources, BLOCK + META, BLOCK)
    return pl.pallas_call(
        spread_kernel,
        out_shape=jax.ShapeDtypeStruct(shape, BF16),
        grid_spec=pltpu.PrefetchScalarGridSpec(
            num_scalar_prefetch=2,
            grid=(1,),
            in_specs=[
                pl.BlockSpec(blocks.shape, lambda i, *_: (0, 0, 0)),
                pl.BlockSpec(meta.shape, lambda i, *_: (0, 0, 0)),
            ],
            out_specs=pl.BlockSpec(shape, lambda i, *_: (0, 0, 0)),
        ),
        compiler_params=pltpu.CompilerParams(vmem_limit_bytes=VMEM_LIMIT),
        cost_estimate=LIGHT,
    )(owner, count, blocks, meta)


def arrange_kernel(order_ref, gate_ref, up_ref, down_ref, gu_ref, dn_ref):
    hid = gate_ref.shape[1]
    gu_ref[:, :hid] = gate_ref[...]
    gu_ref[:, hid:] = up_ref[...]
    dn_ref[...] = down_ref[...]


def arrange(order, gate, up, down):
    width, hid = gate.shape
    n = order.shape[0]
    parts = 2
    step = width // (n * parts)

    def rows(i, order_ref):
        return (order_ref[i // parts] * parts + i % parts, 0)

    def cols(i, order_ref):
        return (0, order_ref[i // parts] * parts + i % parts)

    return pl.pallas_call(
        arrange_kernel,
        out_shape=(
            jax.ShapeDtypeStruct((width, 2 * hid), BF16),
            jax.ShapeDtypeStruct((hid, width), BF16),
        ),
        grid_spec=pltpu.PrefetchScalarGridSpec(
            num_scalar_prefetch=1,
            grid=(n * parts,),
            in_specs=[
                pl.BlockSpec((step, hid), rows),
                pl.BlockSpec((step, hid), rows),
                pl.BlockSpec((hid, step), cols),
            ],
            out_specs=[
                pl.BlockSpec((step, 2 * hid), lambda i, order_ref: (i, 0)),
                pl.BlockSpec((hid, step), lambda i, order_ref: (0, i)),
            ],
        ),
        compiler_params=pltpu.CompilerParams(vmem_limit_bytes=VMEM_LIMIT),
        cost_estimate=LIGHT,
    )(order, gate, up, down)


def patch_kernel(
    factors,
    where_ref,
    scale_ref,
    incoming_ref,
    gate_ref,
    up_ref,
    down_ref,
    gu_in_ref,
    dn_in_ref,
    gu_ref,
    dn_ref,
    blocks,
    held,
    total,
    in_sems,
    out_sems,
    block_sem,
):
    sources = blocks.shape[0]
    load = pltpu.make_async_copy(
        incoming_ref.at[:, pl.ds(0, BLOCK), :], blocks, block_sem.at[0]
    )
    load.start()

    def block_of(ref, row, col):
        return ref.at[
            pl.ds(pl.multiple_of(row * BLOCK, BLOCK), BLOCK),
            pl.ds(pl.multiple_of(col * BLOCK, BLOCK), BLOCK),
        ]

    def fetch(s, ref):
        return pltpu.make_async_copy(
            block_of(ref, where_ref[1, s], where_ref[2, s]), held.at[s], in_sems.at[s]
        )

    def put(s, ref):
        return pltpu.make_async_copy(
            held.at[s], block_of(ref, where_ref[3, s], where_ref[4, s]), out_sems.at[s]
        )

    corner = gate_ref.at[pl.ds(0, BLOCK), pl.ds(0, BLOCK)]

    def arrived(s):
        return pltpu.make_async_copy(corner, held.at[s], in_sems.at[s])

    def written(s):
        return pltpu.make_async_copy(
            held.at[s], gu_ref.at[pl.ds(0, BLOCK), pl.ds(0, BLOCK)], out_sems.at[s]
        )

    def leads(s):
        return where_ref[0, s] == s

    def start(s, carry):
        for m, ref in enumerate((gate_ref, up_ref, down_ref)):

            @pl.when(leads(s) & (where_ref[5, s] == m))
            def _():
                fetch(s, ref).start()

        return carry

    lax.fori_loop(0, sources, start, 0)
    load.wait()

    def add(s, carry):
        first = where_ref[0, s]

        @pl.when(first == s)
        def _():
            total[s] = blocks[s].astype(F32) * scale_ref[s]

        @pl.when((first >= 0) & (first != s))
        def _():
            total[first] = total[first] + blocks[s].astype(F32) * scale_ref[s]

        return carry

    lax.fori_loop(0, sources, add, 0)

    def finish(s, carry):
        @pl.when(leads(s))
        def _():
            arrived(s).wait()
            factor = jnp.where(where_ref[5, s] == 2, F32(factors[1]), F32(factors[0]))
            held[s] = (held[s].astype(F32) + factor * total[s]).astype(BF16)

        @pl.when(leads(s) & (where_ref[5, s] < 2))
        def _():
            put(s, gu_ref).start()

        @pl.when(leads(s) & (where_ref[5, s] == 2))
        def _():
            put(s, dn_ref).start()

        return carry

    lax.fori_loop(0, sources, finish, 0)

    def drain(s, carry):
        @pl.when(leads(s))
        def _():
            written(s).wait()

        return carry

    lax.fori_loop(0, sources, drain, 0)


def patch(factors, where, scale, incoming, gate, up, down, gu, dn):
    sources = incoming.shape[0]
    return pl.pallas_call(
        functools.partial(patch_kernel, factors),
        out_shape=(
            jax.ShapeDtypeStruct(gu.shape, BF16),
            jax.ShapeDtypeStruct(dn.shape, BF16),
        ),
        grid_spec=pltpu.PrefetchScalarGridSpec(
            num_scalar_prefetch=2,
            grid=(1,),
            in_specs=[HBM] * 6,
            out_specs=[HBM, HBM],
            scratch_shapes=[
                pltpu.VMEM((sources, BLOCK, BLOCK), BF16),
                pltpu.VMEM((sources, BLOCK, BLOCK), BF16),
                pltpu.VMEM((sources, BLOCK, BLOCK), F32),
                pltpu.SemaphoreType.DMA((sources,)),
                pltpu.SemaphoreType.DMA((sources,)),
                pltpu.SemaphoreType.DMA((1,)),
            ],
        ),
        input_output_aliases={6: 0, 7: 1},
        compiler_params=pltpu.CompilerParams(vmem_limit_bytes=VMEM_LIMIT),
        cost_estimate=LIGHT,
    )(where, scale, incoming, gate, up, down, gu, dn)


def dot(a, b):
    return jnp.dot(a, b, preferred_element_type=F32)


def weighted(table, rows):
    both = dot(table, rows)
    n = both.shape[0] // 2
    return both[:n] + both[n:]


def two_parts(table):
    high = table.astype(BF16)
    low = (table - high.astype(F32)).astype(BF16)
    return jnp.concatenate([high, low], axis=0)


def silu_product(acc):
    hid = acc.shape[1] // 2
    return (jax.nn.silu(acc[:, :hid]) * acc[:, hid:]).astype(BF16)


def up_kernel(slots, rows_ref, folded_ref, gu_ref, hidden_b_ref, hidden_c_ref, acc_b, acc_c):
    step, steps = pl.program_id(0), pl.num_programs(0)

    @pl.when(step == 0)
    def _():
        acc_b[...] = jnp.zeros_like(acc_b)
        acc_c[...] = jnp.zeros_like(acc_c)

    n = rows_ref.shape[0]
    row = lax.broadcasted_iota(jnp.int32, (n, n), 0)
    col = lax.broadcasted_iota(jnp.int32, (n, n), 1)
    same = (row // slots == col // slots) & (row % (slots // 2) == col % (slots // 2))
    second = (step >= steps // 2).astype(jnp.int32)
    pick = (same & ((col % slots) // (slots // 2) == second)).astype(BF16)
    acc_b[...] += dot(rows_ref[...], gu_ref[...])
    acc_c[...] += dot(dot(pick, folded_ref[...]).astype(BF16), gu_ref[...])

    @pl.when(step == steps - 1)
    def _():
        hidden_b_ref[...] = silu_product(acc_b[...])
        hidden_c_ref[...] = silu_product(acc_c[...])


def up_projection(slots, rows, gu):
    n = rows.shape[0]
    width, wide = gu.shape
    steps = 8
    step = width // steps
    out = jax.ShapeDtypeStruct((n, wide // 2), BF16)
    return pl.pallas_call(
        functools.partial(up_kernel, slots),
        out_shape=(out, out),
        grid=(steps,),
        in_specs=[
            pl.BlockSpec((n, step), lambda k: (0, k)),
            pl.BlockSpec((n, step), lambda k: (0, steps + k % (steps // 2))),
            pl.BlockSpec((step, wide), lambda k: (k, 0)),
        ],
        out_specs=[pl.BlockSpec((n, wide // 2), lambda k: (0, 0))] * 2,
        scratch_shapes=[pltpu.VMEM((n, wide), F32), pltpu.VMEM((n, wide), F32)],
        compiler_params=pltpu.CompilerParams(vmem_limit_bytes=VMEM_LIMIT),
        cost_estimate=LIGHT,
    )(rows, rows, gu)


def down_kernel(slots, hidden_b_ref, hidden_c_ref, dn_ref, dn_second_ref, out_ref):
    step = pl.program_id(0)

    @pl.when(step < 8)
    def _():
        out_ref[...] = dot(hidden_b_ref[...], dn_ref[...]).astype(BF16)

    @pl.when(step >= 8)
    def _():
        first = dot(hidden_c_ref[...], dn_ref[...])
        second = dot(hidden_c_ref[...], dn_second_ref[...])
        row = lax.broadcasted_iota(jnp.int32, first.shape, 0)
        out_ref[...] = jnp.where(row % slots < slots // 2, first, second).astype(BF16)


def down_projection(slots, hidden_b, hidden_c, dn):
    n, hid = hidden_b.shape
    width = dn.shape[1]
    step = width // 8
    return pl.pallas_call(
        functools.partial(down_kernel, slots),
        out_shape=jax.ShapeDtypeStruct((n, width + width // 2), BF16),
        grid=(12,),
        in_specs=[
            pl.BlockSpec((n, hid), lambda k: (0, 0)),
            pl.BlockSpec((n, hid), lambda k: (0, 0)),
            pl.BlockSpec((hid, step), lambda k: (0, k % 8)),
            pl.BlockSpec((hid, step), lambda k: (0, 4 + jnp.maximum(k - 8, 0))),
        ],
        out_specs=pl.BlockSpec((n, step), lambda k: (0, k)),
        compiler_params=pltpu.CompilerParams(vmem_limit_bytes=VMEM_LIMIT),
        cost_estimate=LIGHT,
    )(hidden_b, hidden_c, dn, dn)


def mix_kernel(share_b_ref, share_c_ref, rows_ref, folded_ref, out_ref):
    n = out_ref.shape[1]
    both = dot(share_b_ref[...], rows_ref[...]) + dot(share_c_ref[...], folded_ref[...])
    out_ref[0] = (both[:n] + both[n:]).astype(BF16)


def mix_whole(share_b, share_c, rows):
    n = rows.shape[0]
    width = rows.shape[1] * 2 // 3
    two = share_b.shape[0]
    step = width // 8
    return pl.pallas_call(
        mix_kernel,
        out_shape=jax.ShapeDtypeStruct((4, two // 2, width // 4), BF16),
        grid=(8,),
        in_specs=[
            pl.BlockSpec((two, n), lambda k: (0, 0)),
            pl.BlockSpec((two, n), lambda k: (k // 4, 0)),
            pl.BlockSpec((n, step), lambda k: (0, k)),
            pl.BlockSpec((n, step), lambda k: (0, 8 + k % 4)),
        ],
        out_specs=pl.BlockSpec((1, two // 2, step), lambda k: (k // 2, 0, k % 2)),
        compiler_params=pltpu.CompilerParams(vmem_limit_bytes=VMEM_LIMIT),
        cost_estimate=LIGHT,
    )(share_b, share_c, rows, rows)


def shards(
    tokens,
    routes,
    route_weight,
    gate_weight,
    up_weight,
    down_weight,
    delta_values,
    delta_owner,
    delta_index,
    delta_scale,
    delta_count,
):
    n_expert = lax.axis_size("expert")
    n_group = lax.axis_size("group")
    sources = n_expert * n_group
    me = lax.axis_index("group")
    tok_rows, quarter = tokens.shape
    width, hid = gate_weight.shape[1:]
    listed = delta_owner.shape[1]
    top_count = routes.shape[1]
    capacity = tok_rows * top_count * 9 // (8 * n_expert)
    slots_a = SLOTS_A
    slots_b, slots_c = SLOTS_B, SLOTS_C
    assert slots_a + slots_b + slots_c == capacity and slots_b == 2 * slots_c
    half = width // 2
    gate, up, down = gate_weight[0], up_weight[0], down_weight[0]

    def shift(x, by):
        return lax.ppermute(x, "group", ring(n_group, by))

    def exchange(x, axes):
        return lax.all_to_all(x, axes, split_axis=0, concat_axis=0, tiled=True)

    order = jnp.stack([me, (me + 3) % 4, (me + 1) % 4, (me + 2) % 4]).astype(jnp.int32)
    place = jnp.zeros((4,), jnp.int32).at[order].set(jnp.arange(4, dtype=jnp.int32))

    named = routes[:, :, None] == jnp.arange(n_expert, dtype=jnp.int32)
    member = jnp.any(named, axis=1)
    share = jnp.sum(jnp.where(named, route_weight[:, :, None], 0.0), axis=1)
    before = jnp.tri(tok_rows, k=-1, dtype=BF16)
    rank = dot(before, member.astype(BF16)).astype(jnp.int32)
    rank = jnp.where(member, rank, -1).T
    slot_a = jnp.arange(slots_a, dtype=jnp.int32)
    slot_b = jnp.arange(slots_a, slots_a + slots_b, dtype=jnp.int32)
    slot_c = slots_a + slots_b + slot_b % slots_c
    front = (slot_b - slots_a) < slots_c
    slot_c0, slot_c1 = jnp.where(front, slot_c, -2), jnp.where(front, -2, slot_c)

    def pick(slots):
        hit = rank[:, None, :] == slots[None, :, None]
        return hit.astype(BF16).reshape(n_expert * slots.shape[0], tok_rows)

    def shares(slots):
        hit = rank.T[:, :, None] == slots[None, None, :]
        table = jnp.where(hit, share[:, :, None], 0.0)
        return two_parts(table.reshape(tok_rows, n_expert * slots.shape[0]))

    pick_a = lax.optimization_barrier(pick(slot_a))

    send_a = dot(pick_a, tokens).astype(BF16)
    send_a, tokens = lax.optimization_barrier((send_a, tokens))
    tokens_all = jnp.concatenate(
        [tokens, shift(tokens, 1), shift(tokens, -1), shift(tokens, 2)], axis=1
    )
    recv_a = exchange(send_a.reshape(n_expert, slots_a, quarter), "expert")
    rows_a = recv_a.reshape(n_expert * slots_a, quarter)

    live = jnp.arange(listed, dtype=jnp.int32) < delta_count[0]
    to = (delta_owner[0][None, :] == jnp.arange(sources, dtype=jnp.int32)[:, None]) & live[None, :]
    slot_out = jnp.sum(jnp.where(to, delta_index[0][None, :] + 1, 0), axis=1)
    scale_out = jnp.sum(jnp.where(to, delta_scale[0][None, :], 0), axis=1)
    meta = jnp.stack([slot_out // 8, slot_out % 8, scale_out], axis=1)
    meta = jnp.pad(meta, ((0, 0), (0, META - 3))).astype(BF16)
    meta = jnp.broadcast_to(meta[:, :, None], (sources, META, BLOCK))
    blocks = delta_values.reshape(listed, BLOCK, BLOCK)
    blocks, meta, tokens_all = lax.optimization_barrier((blocks, meta, tokens_all))
    outgoing = spread_blocks(delta_owner[0], delta_count, blocks, meta)
    incoming = exchange(outgoing, ("expert", "group"))

    gu, dn = arrange(order, gate, up, down)

    pick_c = jnp.concatenate([pick(slot_c0), pick(slot_c1)], axis=1)
    share_c = jnp.concatenate([shares(slot_c0), shares(slot_c1)], axis=0)
    tables = (pick(slot_b), pick_c, shares(slot_a), shares(slot_b), share_c)
    pick_b, pick_c, share_a, share_b, share_c = lax.optimization_barrier(tables)
    tokens_all, gu, dn = lax.optimization_barrier((tokens_all, gu, dn))
    send_b = dot(pick_b, tokens_all).astype(BF16)
    halves = jnp.concatenate([tokens_all[:, :half], tokens_all[:, half:]], axis=0)
    send_c = dot(pick_c, halves).astype(BF16)
    send_b = jnp.concatenate([send_b, send_c], axis=1)

    rows = n_expert * slots_a // 2
    after, ahead = shift(rows_a, 1), shift(rows_a, -1)
    far_top, far_bottom = shift(after[:rows], 1), shift(ahead[rows:], -1)

    send_b, incoming = lax.optimization_barrier((send_b, incoming))
    recv_b = exchange(send_b.reshape(n_expert, slots_b, width + half), "expert")
    rows_b = recv_b.reshape(n_expert * slots_b, width + half)

    meta_in = incoming[:, BLOCK : BLOCK + META, 0].astype(jnp.int32)
    slot = meta_in[:, 0] * 8 + meta_in[:, 1] - 1
    scale = jnp.exp2(meta_in[:, 2].astype(F32))
    same = slot[:, None] == slot[None, :]
    entry = jnp.arange(sources, dtype=jnp.int32)
    first = jnp.min(jnp.where(same, entry[None, :], sources), axis=1)
    first = jnp.where(slot >= 0, first, -1)
    row_blocks, col_blocks = width // BLOCK, hid // BLOCK
    per_matrix = row_blocks * col_blocks
    near = row_blocks // n_group
    slot = jnp.maximum(slot, 0)
    matrix = slot // per_matrix
    inside = slot % per_matrix
    is_down = matrix == 2
    wide = jnp.where(is_down, inside % row_blocks, inside // col_blocks)
    narrow = jnp.where(is_down, inside // row_blocks, inside % col_blocks)
    moved = place[wide // near] * near + wide % near
    where = jnp.stack(
        [
            first,
            jnp.where(is_down, narrow, wide),
            jnp.where(is_down, wide, narrow),
            jnp.where(is_down, narrow, moved),
            jnp.where(is_down, moved, narrow + col_blocks * (matrix == 1)),
            matrix,
        ]
    ).astype(jnp.int32)
    factors = (width**-0.5, (hid * n_group) ** -0.5)
    gu, dn = patch(factors, where, scale, incoming, gate, up, down, gu, dn)

    acc = dot(rows_a, gu[:quarter])
    acc = acc + dot(after, gu[quarter : 2 * quarter])
    acc = acc + dot(ahead, gu[2 * quarter : 3 * quarter])
    acc, far_top, far_bottom = lax.optimization_barrier((acc, far_top, far_bottom))
    last = gu[3 * quarter :]
    hidden_top = silu_product(acc[:rows] + dot(far_top, last))
    hidden_bottom = silu_product(acc[rows:] + dot(far_bottom, last))

    def part(hidden, index):
        return dot(hidden, dn[:, index * quarter : (index + 1) * quarter])

    top_3, bottom_3 = part(hidden_top, 3).astype(BF16), part(hidden_bottom, 3).astype(BF16)
    top_3, bottom_3, rows_b = lax.optimization_barrier((top_3, bottom_3, rows_b))
    top_3, bottom_3 = shift(top_3, -1), shift(bottom_3, 1)

    hidden_b, hidden_c = up_projection(slots_b, rows_b, gu)
    part_b = down_projection(slots_b, hidden_b, hidden_c, dn)
    back_b = exchange(part_b.reshape(n_expert, slots_b, width + half), "expert")

    hidden_a = jnp.concatenate([hidden_top, hidden_bottom], axis=0)
    part_1, part_2 = part(hidden_a, 1), part(hidden_a, 2)
    none = jnp.zeros_like(top_3)
    part_1 = (part_1 + jnp.concatenate([top_3, none], axis=0).astype(F32)).astype(BF16)
    part_2 = (part_2 + jnp.concatenate([none, bottom_3], axis=0).astype(F32)).astype(BF16)
    part_1, part_2 = shift(part_1, -1), shift(part_2, 1)
    out_a = part(hidden_a, 0) + part_1.astype(F32) + part_2.astype(F32)
    out_a, back_b = lax.optimization_barrier((out_a.astype(BF16), back_b))
    back_a = exchange(out_a.reshape(n_expert, slots_a, quarter), "expert")

    mix_b = mix_whole(share_b, share_c, back_b.reshape(n_expert * slots_b, width + half))
    result = mix_b[0].astype(F32)
    for i, by in ((1, -1), (2, 1), (3, 2)):
        result = result + shift(mix_b[i], by).astype(F32)
    mix_a = weighted(share_a, back_a.reshape(n_expert * slots_a, quarter))
    return (result + mix_a).astype(BF16)


def solution(mesh):
    return jax.shard_map(
        shards,
        mesh=mesh,
        in_specs=(
            P("expert", "group"),
            P("expert", None),
            P("expert", None),
            P("expert", None, "group"),
            P("expert", None, "group"),
            P("expert", "group", None),
            P(("expert", "group"), None),
            P(("expert", "group"), None),
            P(("expert", "group"), None),
            P(("expert", "group"), None),
            P(("expert", "group")),
        ),
        out_specs=P("expert", "group"),
        check_vma=False,
    )
```

```python
import functools

import jax
import jax.numpy as jnp
from jax import lax
from jax.experimental import pallas as pl
from jax.experimental.pallas import tpu as pltpu
from jax.sharding import PartitionSpec as P

BLOCK = 128
META = 16
SLOTS_A = 24
SLOTS_B = 8
SLOTS_C = 4
VMEM_LIMIT = 60 * 2**20
BF16 = jnp.bfloat16
F32 = jnp.float32
LIGHT = pl.CostEstimate(flops=0, bytes_accessed=0, transcendentals=0)
HBM = pl.BlockSpec(memory_space=pltpu.HBM)


def ring(n, shift):
    return [(i, (i + shift) % n) for i in range(n)]


def spread_kernel(owner_ref, count_ref, blocks_ref, meta_ref, out_ref):
    out_ref[:, BLOCK:, :] = meta_ref[...]

    def put(i, carry):
        out_ref[owner_ref[i], :BLOCK, :] = blocks_ref[i]
        return carry

    lax.fori_loop(0, count_ref[0], put, 0)


def spread_blocks(owner, count, blocks, meta):
    sources = meta.shape[0]
    shape = (sources, BLOCK + META, BLOCK)
    return pl.pallas_call(
        spread_kernel,
        out_shape=jax.ShapeDtypeStruct(shape, BF16),
        grid_spec=pltpu.PrefetchScalarGridSpec(
            num_scalar_prefetch=2,
            grid=(1,),
            in_specs=[
                pl.BlockSpec(blocks.shape, lambda i, *_: (0, 0, 0)),
                pl.BlockSpec(meta.shape, lambda i, *_: (0, 0, 0)),
            ],
            out_specs=pl.BlockSpec(shape, lambda i, *_: (0, 0, 0)),
        ),
        compiler_params=pltpu.CompilerParams(vmem_limit_bytes=VMEM_LIMIT),
        cost_estimate=LIGHT,
    )(owner, count, blocks, meta)


def arrange_kernel(order_ref, gate_ref, up_ref, down_ref, gu_ref, dn_ref):
    hid = gate_ref.shape[1]
    gu_ref[:, :hid] = gate_ref[...]
    gu_ref[:, hid:] = up_ref[...]
    dn_ref[...] = down_ref[...]


def arrange(order, gate, up, down):
    width, hid = gate.shape
    n = order.shape[0]
    parts = 2
    step = width // (n * parts)

    def rows(i, order_ref):
        return (order_ref[i // parts] * parts + i % parts, 0)

    def cols(i, order_ref):
        return (0, order_ref[i // parts] * parts + i % parts)

    return pl.pallas_call(
        arrange_kernel,
        out_shape=(
            jax.ShapeDtypeStruct((width, 2 * hid), BF16),
            jax.ShapeDtypeStruct((hid, width), BF16),
        ),
        grid_spec=pltpu.PrefetchScalarGridSpec(
            num_scalar_prefetch=1,
            grid=(n * parts,),
            in_specs=[
                pl.BlockSpec((step, hid), rows),
                pl.BlockSpec((step, hid), rows),
                pl.BlockSpec((hid, step), cols),
            ],
            out_specs=[
                pl.BlockSpec((step, 2 * hid), lambda i, order_ref: (i, 0)),
                pl.BlockSpec((hid, step), lambda i, order_ref: (0, i)),
            ],
        ),
        compiler_params=pltpu.CompilerParams(vmem_limit_bytes=VMEM_LIMIT),
        cost_estimate=LIGHT,
    )(order, gate, up, down)


def patch_kernel(
    factors,
    where_ref,
    scale_ref,
    incoming_ref,
    gate_ref,
    up_ref,
    down_ref,
    gu_in_ref,
    dn_in_ref,
    gu_ref,
    dn_ref,
    blocks,
    held,
    total,
    in_sems,
    out_sems,
    block_sem,
):
    sources = blocks.shape[0]
    load = pltpu.make_async_copy(
        incoming_ref.at[:, pl.ds(0, BLOCK), :], blocks, block_sem.at[0]
    )
    load.start()

    def block_of(ref, row, col):
        return ref.at[
            pl.ds(pl.multiple_of(row * BLOCK, BLOCK), BLOCK),
            pl.ds(pl.multiple_of(col * BLOCK, BLOCK), BLOCK),
        ]

    def fetch(s, ref):
        return pltpu.make_async_copy(
            block_of(ref, where_ref[1, s], where_ref[2, s]), held.at[s], in_sems.at[s]
        )

    def put(s, ref):
        return pltpu.make_async_copy(
            held.at[s], block_of(ref, where_ref[3, s], where_ref[4, s]), out_sems.at[s]
        )

    corner = gate_ref.at[pl.ds(0, BLOCK), pl.ds(0, BLOCK)]

    def arrived(s):
        return pltpu.make_async_copy(corner, held.at[s], in_sems.at[s])

    def written(s):
        return pltpu.make_async_copy(
            held.at[s], gu_ref.at[pl.ds(0, BLOCK), pl.ds(0, BLOCK)], out_sems.at[s]
        )

    def leads(s):
        return where_ref[0, s] == s

    def start(s, carry):
        for m, ref in enumerate((gate_ref, up_ref, down_ref)):

            @pl.when(leads(s) & (where_ref[5, s] == m))
            def _():
                fetch(s, ref).start()

        return carry

    lax.fori_loop(0, sources, start, 0)
    load.wait()

    def add(s, carry):
        first = where_ref[0, s]

        @pl.when(first == s)
        def _():
            total[s] = blocks[s].astype(F32) * scale_ref[s]

        @pl.when((first >= 0) & (first != s))
        def _():
            total[first] = total[first] + blocks[s].astype(F32) * scale_ref[s]

        return carry

    lax.fori_loop(0, sources, add, 0)

    def finish(s, carry):
        @pl.when(leads(s))
        def _():
            arrived(s).wait()
            factor = jnp.where(where_ref[5, s] == 2, F32(factors[1]), F32(factors[0]))
            held[s] = (held[s].astype(F32) + factor * total[s]).astype(BF16)

        @pl.when(leads(s) & (where_ref[5, s] < 2))
        def _():
            put(s, gu_ref).start()

        @pl.when(leads(s) & (where_ref[5, s] == 2))
        def _():
            put(s, dn_ref).start()

        return carry

    lax.fori_loop(0, sources, finish, 0)

    def drain(s, carry):
        @pl.when(leads(s))
        def _():
            written(s).wait()

        return carry

    lax.fori_loop(0, sources, drain, 0)


def patch(factors, where, scale, incoming, gate, up, down, gu, dn):
    sources = incoming.shape[0]
    return pl.pallas_call(
        functools.partial(patch_kernel, factors),
        out_shape=(
            jax.ShapeDtypeStruct(gu.shape, BF16),
            jax.ShapeDtypeStruct(dn.shape, BF16),
        ),
        grid_spec=pltpu.PrefetchScalarGridSpec(
            num_scalar_prefetch=2,
            grid=(1,),
            in_specs=[HBM] * 6,
            out_specs=[HBM, HBM],
            scratch_shapes=[
                pltpu.VMEM((sources, BLOCK, BLOCK), BF16),
                pltpu.VMEM((sources, BLOCK, BLOCK), BF16),
                pltpu.VMEM((sources, BLOCK, BLOCK), F32),
                pltpu.SemaphoreType.DMA((sources,)),
                pltpu.SemaphoreType.DMA((sources,)),
                pltpu.SemaphoreType.DMA((1,)),
            ],
        ),
        input_output_aliases={6: 0, 7: 1},
        compiler_params=pltpu.CompilerParams(vmem_limit_bytes=VMEM_LIMIT),
        cost_estimate=LIGHT,
    )(where, scale, incoming, gate, up, down, gu, dn)


def dot(a, b):
    return jnp.dot(a, b, preferred_element_type=F32)


def weighted(table, rows):
    both = dot(table, rows)
    n = both.shape[0] // 2
    return both[:n] + both[n:]


def two_parts(table):
    high = table.astype(BF16)
    low = (table - high.astype(F32)).astype(BF16)
    return jnp.concatenate([high, low], axis=0)


def silu_product(acc):
    hid = acc.shape[1] // 2
    return (jax.nn.silu(acc[:, :hid]) * acc[:, hid:]).astype(BF16)


def up_kernel(slots, rows_ref, folded_ref, gu_ref, hidden_b_ref, hidden_c_ref, acc, rows, pick):
    step, steps = pl.program_id(0), pl.num_programs(0)
    n = rows_ref.shape[0]

    @pl.when(step == 0)
    def _():
        acc[...] = jnp.zeros_like(acc)

    @pl.when((step == 0) | (step == steps // 2))
    def _():
        row = lax.broadcasted_iota(jnp.int32, (n, n), 0)
        col = lax.broadcasted_iota(jnp.int32, (n, n), 1)
        same = (row // slots == col // slots) & (row % (slots // 2) == col % (slots // 2))
        second = (step >= steps // 2).astype(jnp.int32)
        here = same & ((col % slots) // (slots // 2) == second)
        pick[...] = jnp.where(here, 1.0, 0.0).astype(BF16)

    rows[:n] = rows_ref[...]
    rows[n:] = dot(pick[...], folded_ref[...]).astype(BF16)
    acc[...] += dot(rows[...], gu_ref[...])

    @pl.when(step == steps - 1)
    def _():
        hidden_b_ref[...] = silu_product(acc[:n])
        hidden_c_ref[...] = silu_product(acc[n:])


def up_projection(slots, rows, gu):
    n = rows.shape[0]
    width, wide = gu.shape
    steps = 4
    step = width // steps
    out = jax.ShapeDtypeStruct((n, wide // 2), BF16)
    return pl.pallas_call(
        functools.partial(up_kernel, slots),
        out_shape=(out, out),
        grid=(steps,),
        in_specs=[
            pl.BlockSpec((n, step), lambda k: (0, k)),
            pl.BlockSpec((n, step), lambda k: (0, steps + k % (steps // 2))),
            pl.BlockSpec((step, wide), lambda k: (k, 0)),
        ],
        out_specs=[pl.BlockSpec((n, wide // 2), lambda k: (0, 0))] * 2,
        scratch_shapes=[
            pltpu.VMEM((2 * n, wide), F32),
            pltpu.VMEM((2 * n, step), BF16),
            pltpu.VMEM((n, n), BF16),
        ],
        compiler_params=pltpu.CompilerParams(vmem_limit_bytes=VMEM_LIMIT),
        cost_estimate=LIGHT,
    )(rows, rows, gu)


def down_kernel(slots, hidden_b_ref, hidden_c_ref, dn_ref, dn_second_ref, out_ref):
    step = dn_ref.shape[1]
    hidden_c = hidden_c_ref[...]
    row = lax.broadcasted_iota(jnp.int32, (hidden_c.shape[0], step), 0)
    out_ref[:, :step] = dot(hidden_b_ref[...], dn_ref[...]).astype(BF16)
    out_ref[:, step : 2 * step] = dot(hidden_b_ref[...], dn_second_ref[...]).astype(BF16)
    first, second = dot(hidden_c, dn_ref[...]), dot(hidden_c, dn_second_ref[...])
    folded = jnp.where(row % slots < slots // 2, first, second)
    out_ref[:, 2 * step :] = folded.astype(BF16)


def down_projection(slots, hidden_b, hidden_c, dn):
    n, hid = hidden_b.shape
    width = dn.shape[1]
    step = width // 8
    return pl.pallas_call(
        functools.partial(down_kernel, slots),
        out_shape=jax.ShapeDtypeStruct((n, 12 * step), BF16),
        grid=(4,),
        in_specs=[
            pl.BlockSpec((n, hid), lambda k: (0, 0)),
            pl.BlockSpec((n, hid), lambda k: (0, 0)),
            pl.BlockSpec((hid, step), lambda k: (0, k)),
            pl.BlockSpec((hid, step), lambda k: (0, 4 + k)),
        ],
        out_specs=pl.BlockSpec((n, 3 * step), lambda k: (0, k)),
        compiler_params=pltpu.CompilerParams(vmem_limit_bytes=VMEM_LIMIT),
        cost_estimate=LIGHT,
    )(hidden_b, hidden_c, dn, dn)


def mix_kernel(share_b_ref, share_c_ref, rows_ref, folded_ref, out_ref):
    n = out_ref.shape[1]
    both = dot(share_b_ref[...], rows_ref[...]) + dot(share_c_ref[...], folded_ref[...])
    out_ref[0] = (both[:n] + both[n:]).astype(BF16)


def mix_whole(share_b, share_c, rows):
    n = rows.shape[0]
    width = rows.shape[1] * 2 // 3
    two = share_b.shape[0]
    step = width // 8
    return pl.pallas_call(
        mix_kernel,
        out_shape=jax.ShapeDtypeStruct((4, two // 2, width // 4), BF16),
        grid=(8,),
        in_specs=[
            pl.BlockSpec((two, n), lambda k: (0, 0)),
            pl.BlockSpec((two, n), lambda k: (k // 4, 0)),
            pl.BlockSpec((n, step), lambda k: (0, 3 * (k % 4) + k // 4)),
            pl.BlockSpec((n, step), lambda k: (0, 3 * (k % 4) + 2)),
        ],
        out_specs=pl.BlockSpec((1, two // 2, step), lambda k: (k // 2, 0, k % 2)),
        compiler_params=pltpu.CompilerParams(vmem_limit_bytes=VMEM_LIMIT),
        cost_estimate=LIGHT,
    )(share_b, share_c, rows, rows)


def shards(
    tokens,
    routes,
    route_weight,
    gate_weight,
    up_weight,
    down_weight,
    delta_values,
    delta_owner,
    delta_index,
    delta_scale,
    delta_count,
):
    n_expert = lax.axis_size("expert")
    n_group = lax.axis_size("group")
    sources = n_expert * n_group
    me = lax.axis_index("group")
    tok_rows, quarter = tokens.shape
    width, hid = gate_weight.shape[1:]
    listed = delta_owner.shape[1]
    top_count = routes.shape[1]
    capacity = tok_rows * top_count * 9 // (8 * n_expert)
    slots_a = SLOTS_A
    slots_b, slots_c = SLOTS_B, SLOTS_C
    assert slots_a + slots_b + slots_c == capacity and slots_b == 2 * slots_c
    half = width // 2
    gate, up, down = gate_weight[0], up_weight[0], down_weight[0]

    def shift(x, by):
        return lax.ppermute(x, "group", ring(n_group, by))

    def exchange(x, axes):
        return lax.all_to_all(x, axes, split_axis=0, concat_axis=0, tiled=True)

    order = jnp.stack([me, (me + 3) % 4, (me + 1) % 4, (me + 2) % 4]).astype(jnp.int32)

    named = routes[:, :, None] == jnp.arange(n_expert, dtype=jnp.int32)
    member = jnp.any(named, axis=1)
    share = jnp.sum(jnp.where(named, route_weight[:, :, None], 0.0), axis=1)
    before = jnp.tri(tok_rows, k=-1, dtype=BF16)
    rank = dot(before, member.astype(BF16)).astype(jnp.int32)
    rank = jnp.where(member, rank, -1).T
    slot_a = jnp.arange(slots_a, dtype=jnp.int32)
    slot_b = jnp.arange(slots_a, slots_a + slots_b, dtype=jnp.int32)
    slot_c = slots_a + slots_b + slot_b % slots_c
    front = (slot_b - slots_a) < slots_c
    slot_c0, slot_c1 = jnp.where(front, slot_c, -2), jnp.where(front, -2, slot_c)

    def pick(slots):
        hit = rank[:, None, :] == slots[None, :, None]
        return hit.astype(BF16).reshape(n_expert * slots.shape[0], tok_rows)

    def shares(slots):
        hit = rank.T[:, :, None] == slots[None, None, :]
        table = jnp.where(hit, share[:, :, None], 0.0)
        return two_parts(table.reshape(tok_rows, n_expert * slots.shape[0]))

    pick_a = lax.optimization_barrier(pick(slot_a))

    send_a = dot(pick_a, tokens).astype(BF16)
    send_a, tokens = lax.optimization_barrier((send_a, tokens))
    tokens_all = jnp.concatenate(
        [tokens, shift(tokens, 1), shift(tokens, -1), shift(tokens, 2)], axis=1
    )
    recv_a = exchange(send_a.reshape(n_expert, slots_a, quarter), "expert")
    rows_a = recv_a.reshape(n_expert * slots_a, quarter)

    live = jnp.arange(listed, dtype=jnp.int32) < delta_count[0]
    to = (delta_owner[0][None, :] == jnp.arange(sources, dtype=jnp.int32)[:, None]) & live[None, :]
    slot_out = jnp.sum(jnp.where(to, delta_index[0][None, :] + 1, 0), axis=1)
    scale_out = jnp.sum(jnp.where(to, delta_scale[0][None, :], 0), axis=1)
    meta = jnp.stack([slot_out // 8, slot_out % 8, scale_out], axis=1)
    meta = jnp.pad(meta, ((0, 0), (0, META - 3))).astype(BF16)
    meta = jnp.broadcast_to(meta[:, :, None], (sources, META, BLOCK))
    blocks = delta_values.reshape(listed, BLOCK, BLOCK)
    blocks, meta, tokens_all = lax.optimization_barrier((blocks, meta, tokens_all))
    outgoing = spread_blocks(delta_owner[0], delta_count, blocks, meta)
    incoming = exchange(outgoing, ("expert", "group"))

    gu, dn = arrange(order, gate, up, down)

    pick_c = jnp.concatenate([pick(slot_c0), pick(slot_c1)], axis=1)
    share_c = jnp.concatenate([shares(slot_c0), shares(slot_c1)], axis=0)
    tables = (pick(slot_b), pick_c, shares(slot_a), shares(slot_b), share_c)
    pick_b, pick_c, share_a, share_b, share_c = lax.optimization_barrier(tables)
    tokens_all, gu, dn = lax.optimization_barrier((tokens_all, gu, dn))
    send_b = dot(pick_b, tokens_all).astype(BF16)
    halves = jnp.concatenate([tokens_all[:, :half], tokens_all[:, half:]], axis=0)
    send_c = dot(pick_c, halves).astype(BF16)
    send_b = jnp.concatenate([send_b, send_c], axis=1)

    rows = n_expert * slots_a // 2
    after, ahead = shift(rows_a, 1), shift(rows_a, -1)
    far_top, far_bottom = shift(after[:rows], 1), shift(ahead[rows:], -1)

    send_b, incoming = lax.optimization_barrier((send_b, incoming))
    recv_b = exchange(send_b.reshape(n_expert, slots_b, width + half), "expert")
    rows_b = recv_b.reshape(n_expert * slots_b, width + half)

    meta_in = incoming[:, BLOCK : BLOCK + META, 0].astype(jnp.int32)
    slot = meta_in[:, 0] * 8 + meta_in[:, 1] - 1
    scale = jnp.exp2(meta_in[:, 2].astype(F32))
    same = slot[:, None] == slot[None, :]
    entry = jnp.arange(sources, dtype=jnp.int32)
    first = jnp.min(jnp.where(same, entry[None, :], sources), axis=1)
    first = jnp.where(slot >= 0, first, -1)
    row_blocks, col_blocks = width // BLOCK, hid // BLOCK
    per_matrix = row_blocks * col_blocks
    near = row_blocks // n_group
    slot = jnp.maximum(slot, 0)
    matrix = slot // per_matrix
    inside = slot % per_matrix
    is_down = matrix == 2
    wide = jnp.where(is_down, inside % row_blocks, inside // col_blocks)
    narrow = jnp.where(is_down, inside // row_blocks, inside % col_blocks)
    distance = (wide // near - me + n_group) % n_group
    place = jnp.where(distance == 0, 0, jnp.where(distance == 3, 1, distance + 1))
    moved = place * near + wide % near
    where = jnp.stack(
        [
            first,
            jnp.where(is_down, narrow, wide),
            jnp.where(is_down, wide, narrow),
            jnp.where(is_down, narrow, moved),
            jnp.where(is_down, moved, narrow + col_blocks * (matrix == 1)),
            matrix,
        ]
    ).astype(jnp.int32)
    factors = (width**-0.5, (hid * n_group) ** -0.5)
    gu, dn = patch(factors, where, scale, incoming, gate, up, down, gu, dn)

    acc = dot(rows_a, gu[:quarter])
    acc = acc + dot(after, gu[quarter : 2 * quarter])
    acc = acc + dot(ahead, gu[2 * quarter : 3 * quarter])
    acc, far_top, far_bottom = lax.optimization_barrier((acc, far_top, far_bottom))
    last = gu[3 * quarter :]
    hidden_top = silu_product(acc[:rows] + dot(far_top, last))
    hidden_bottom = silu_product(acc[rows:] + dot(far_bottom, last))

    def part(hidden, index):
        return dot(hidden, dn[:, index * quarter : (index + 1) * quarter])

    top_3, bottom_3 = part(hidden_top, 3).astype(BF16), part(hidden_bottom, 3).astype(BF16)
    top_3, bottom_3, rows_b = lax.optimization_barrier((top_3, bottom_3, rows_b))
    top_3, bottom_3 = shift(top_3, -1), shift(bottom_3, 1)

    hidden_b, hidden_c = up_projection(slots_b, rows_b, gu)
    part_b = down_projection(slots_b, hidden_b, hidden_c, dn)
    back_b = exchange(part_b.reshape(n_expert, slots_b, width + half), "expert")

    hidden_a = jnp.concatenate([hidden_top, hidden_bottom], axis=0)
    part_1, part_2 = part(hidden_a, 1), part(hidden_a, 2)
    none = jnp.zeros_like(top_3)
    part_1 = (part_1 + jnp.concatenate([top_3, none], axis=0).astype(F32)).astype(BF16)
    part_2 = (part_2 + jnp.concatenate([none, bottom_3], axis=0).astype(F32)).astype(BF16)
    part_1, part_2 = shift(part_1, -1), shift(part_2, 1)
    out_a = part(hidden_a, 0) + part_1.astype(F32) + part_2.astype(F32)
    out_a, back_b = lax.optimization_barrier((out_a.astype(BF16), back_b))
    back_a = exchange(out_a.reshape(n_expert, slots_a, quarter), "expert")

    mix_b = mix_whole(share_b, share_c, back_b.reshape(n_expert * slots_b, width + half))
    result = mix_b[0].astype(F32)
    for i, by in ((1, -1), (2, 1), (3, 2)):
        result = result + shift(mix_b[i], by).astype(F32)
    mix_a = weighted(share_a, back_a.reshape(n_expert * slots_a, quarter))
    return (result + mix_a).astype(BF16)


def solution(mesh):
    return jax.shard_map(
        shards,
        mesh=mesh,
        in_specs=(
            P("expert", "group"),
            P("expert", None),
            P("expert", None),
            P("expert", None, "group"),
            P("expert", None, "group"),
            P("expert", "group", None),
            P(("expert", "group"), None),
            P(("expert", "group"), None),
            P(("expert", "group"), None),
            P(("expert", "group"), None),
            P(("expert", "group")),
        ),
        out_specs=P("expert", "group"),
        check_vma=False,
    )
```

```python
import functools

import jax
import jax.numpy as jnp
from jax import lax
from jax.experimental import pallas as pl
from jax.experimental.pallas import tpu as pltpu
from jax.sharding import PartitionSpec as P

BLOCK = 128
META = 8
SLOTS_A = 24
SLOTS_B = 8
SLOTS_C = 4
VMEM_LIMIT = 60 * 2**20
BF16 = jnp.bfloat16
F32 = jnp.float32
LIGHT = pl.CostEstimate(flops=0, bytes_accessed=0, transcendentals=0)
HBM = pl.BlockSpec(memory_space=pltpu.HBM)


def ring(n, shift):
    return [(i, (i + shift) % n) for i in range(n)]


def spread_kernel(owner_ref, count_ref, blocks_ref, meta_ref, out_ref):
    out_ref[:, BLOCK:, :] = meta_ref[...]

    def put(i, carry):
        out_ref[owner_ref[i], :BLOCK, :] = blocks_ref[i]
        return carry

    lax.fori_loop(0, count_ref[0], put, 0)


def spread_blocks(owner, count, blocks, meta):
    sources = meta.shape[0]
    shape = (sources, BLOCK + META, BLOCK)
    return pl.pallas_call(
        spread_kernel,
        out_shape=jax.ShapeDtypeStruct(shape, BF16),
        grid_spec=pltpu.PrefetchScalarGridSpec(
            num_scalar_prefetch=2,
            grid=(1,),
            in_specs=[
                pl.BlockSpec(blocks.shape, lambda i, *_: (0, 0, 0)),
                pl.BlockSpec(meta.shape, lambda i, *_: (0, 0, 0)),
            ],
            out_specs=pl.BlockSpec(shape, lambda i, *_: (0, 0, 0)),
        ),
        compiler_params=pltpu.CompilerParams(vmem_limit_bytes=VMEM_LIMIT),
        cost_estimate=LIGHT,
    )(owner, count, blocks, meta)


def arrange_kernel(order_ref, gate_ref, up_ref, down_ref, gu_ref, dn_ref):
    hid = gate_ref.shape[1]
    gu_ref[:, :hid] = gate_ref[...]
    gu_ref[:, hid:] = up_ref[...]
    dn_ref[...] = down_ref[...]


def arrange(order, gate, up, down):
    width, hid = gate.shape
    n = order.shape[0]
    parts = 2
    step = width // (n * parts)

    def rows(i, order_ref):
        return (order_ref[i // parts] * parts + i % parts, 0)

    def cols(i, order_ref):
        return (0, order_ref[i // parts] * parts + i % parts)

    return pl.pallas_call(
        arrange_kernel,
        out_shape=(
            jax.ShapeDtypeStruct((width, 2 * hid), BF16),
            jax.ShapeDtypeStruct((hid, width), BF16),
        ),
        grid_spec=pltpu.PrefetchScalarGridSpec(
            num_scalar_prefetch=1,
            grid=(n * parts,),
            in_specs=[
                pl.BlockSpec((step, hid), rows),
                pl.BlockSpec((step, hid), rows),
                pl.BlockSpec((hid, step), cols),
            ],
            out_specs=[
                pl.BlockSpec((step, 2 * hid), lambda i, order_ref: (i, 0)),
                pl.BlockSpec((hid, step), lambda i, order_ref: (0, i)),
            ],
        ),
        compiler_params=pltpu.CompilerParams(vmem_limit_bytes=VMEM_LIMIT),
        cost_estimate=LIGHT,
    )(order, gate, up, down)


def patch_kernel(
    factors,
    where_ref,
    scale_ref,
    incoming_ref,
    gate_ref,
    up_ref,
    down_ref,
    gu_in_ref,
    dn_in_ref,
    gu_ref,
    dn_ref,
    blocks,
    held,
    total,
    in_sems,
    out_sems,
    block_sem,
):
    sources = blocks.shape[0]
    load = pltpu.make_async_copy(
        incoming_ref.at[:, pl.ds(0, BLOCK), :], blocks, block_sem.at[0]
    )
    load.start()

    def block_of(ref, row, col):
        return ref.at[
            pl.ds(pl.multiple_of(row * BLOCK, BLOCK), BLOCK),
            pl.ds(pl.multiple_of(col * BLOCK, BLOCK), BLOCK),
        ]

    def fetch(s, ref):
        return pltpu.make_async_copy(
            block_of(ref, where_ref[1, s], where_ref[2, s]), held.at[s], in_sems.at[s]
        )

    def put(s, ref):
        return pltpu.make_async_copy(
            held.at[s], block_of(ref, where_ref[3, s], where_ref[4, s]), out_sems.at[s]
        )

    corner = gate_ref.at[pl.ds(0, BLOCK), pl.ds(0, BLOCK)]

    def arrived(s):
        return pltpu.make_async_copy(corner, held.at[s], in_sems.at[s])

    def written(s):
        return pltpu.make_async_copy(
            held.at[s], gu_ref.at[pl.ds(0, BLOCK), pl.ds(0, BLOCK)], out_sems.at[s]
        )

    def leads(s):
        return where_ref[0, s] == s

    def start(s, carry):
        for m, ref in enumerate((gate_ref, up_ref, down_ref)):

            @pl.when(leads(s) & (where_ref[5, s] == m))
            def _():
                fetch(s, ref).start()

        return carry

    lax.fori_loop(0, sources, start, 0)
    load.wait()

    def add(s, carry):
        first = where_ref[0, s]

        @pl.when(first == s)
        def _():
            total[s] = blocks[s].astype(F32) * scale_ref[s]

        @pl.when((first >= 0) & (first != s))
        def _():
            total[first] = total[first] + blocks[s].astype(F32) * scale_ref[s]

        return carry

    lax.fori_loop(0, sources, add, 0)

    def finish(s, carry):
        @pl.when(leads(s))
        def _():
            arrived(s).wait()
            factor = jnp.where(where_ref[5, s] == 2, F32(factors[1]), F32(factors[0]))
            held[s] = (held[s].astype(F32) + factor * total[s]).astype(BF16)

        @pl.when(leads(s) & (where_ref[5, s] < 2))
        def _():
            put(s, gu_ref).start()

        @pl.when(leads(s) & (where_ref[5, s] == 2))
        def _():
            put(s, dn_ref).start()

        return carry

    lax.fori_loop(0, sources, finish, 0)

    def drain(s, carry):
        @pl.when(leads(s))
        def _():
            written(s).wait()

        return carry

    lax.fori_loop(0, sources, drain, 0)


def patch(factors, where, scale, incoming, gate, up, down, gu, dn):
    sources = incoming.shape[0]
    return pl.pallas_call(
        functools.partial(patch_kernel, factors),
        out_shape=(
            jax.ShapeDtypeStruct(gu.shape, BF16),
            jax.ShapeDtypeStruct(dn.shape, BF16),
        ),
        grid_spec=pltpu.PrefetchScalarGridSpec(
            num_scalar_prefetch=2,
            grid=(1,),
            in_specs=[HBM] * 6,
            out_specs=[HBM, HBM],
            scratch_shapes=[
                pltpu.VMEM((sources, BLOCK, BLOCK), BF16),
                pltpu.VMEM((sources, BLOCK, BLOCK), BF16),
                pltpu.VMEM((sources, BLOCK, BLOCK), F32),
                pltpu.SemaphoreType.DMA((sources,)),
                pltpu.SemaphoreType.DMA((sources,)),
                pltpu.SemaphoreType.DMA((1,)),
            ],
        ),
        input_output_aliases={6: 0, 7: 1},
        compiler_params=pltpu.CompilerParams(vmem_limit_bytes=VMEM_LIMIT),
        cost_estimate=LIGHT,
    )(where, scale, incoming, gate, up, down, gu, dn)


def dot(a, b):
    return jnp.dot(a, b, preferred_element_type=F32)


def weighted(table, rows):
    both = dot(table, rows)
    n = both.shape[0] // 2
    return both[:n] + both[n:]


def two_parts(table):
    high = table.astype(BF16)
    low = (table - high.astype(F32)).astype(BF16)
    return jnp.concatenate([high, low], axis=0)


def silu_product(acc):
    hid = acc.shape[1] // 2
    return (jax.nn.silu(acc[:, :hid]) * acc[:, hid:]).astype(BF16)


def up_kernel(slots, rows_ref, folded_ref, gu_ref, hidden_b_ref, hidden_c_ref, acc, rows, pick):
    step, steps = pl.program_id(0), pl.num_programs(0)
    n = rows_ref.shape[0]

    @pl.when(step == 0)
    def _():
        acc[...] = jnp.zeros_like(acc)

    @pl.when((step == 0) | (step == steps // 2))
    def _():
        row = lax.broadcasted_iota(jnp.int32, (n, n), 0)
        col = lax.broadcasted_iota(jnp.int32, (n, n), 1)
        same = (row // slots == col // slots) & (row % (slots // 2) == col % (slots // 2))
        second = (step >= steps // 2).astype(jnp.int32)
        here = same & ((col % slots) // (slots // 2) == second)
        pick[...] = jnp.where(here, 1.0, 0.0).astype(BF16)

    rows[:n] = rows_ref[...]
    rows[n:] = dot(pick[...], folded_ref[...]).astype(BF16)
    acc[...] += dot(rows[...], gu_ref[...])

    @pl.when(step == steps - 1)
    def _():
        hidden_b_ref[...] = silu_product(acc[:n])
        hidden_c_ref[...] = silu_product(acc[n:])


def up_projection(slots, rows, gu):
    n = rows.shape[0]
    width, wide = gu.shape
    steps = 4
    step = width // steps
    out = jax.ShapeDtypeStruct((n, wide // 2), BF16)
    return pl.pallas_call(
        functools.partial(up_kernel, slots),
        out_shape=(out, out),
        grid=(steps,),
        in_specs=[
            pl.BlockSpec((n, step), lambda k: (0, k)),
            pl.BlockSpec((n, step), lambda k: (0, steps + k % (steps // 2))),
            pl.BlockSpec((step, wide), lambda k: (k, 0)),
        ],
        out_specs=[pl.BlockSpec((n, wide // 2), lambda k: (0, 0))] * 2,
        scratch_shapes=[
            pltpu.VMEM((2 * n, wide), F32),
            pltpu.VMEM((2 * n, step), BF16),
            pltpu.VMEM((n, n), BF16),
        ],
        compiler_params=pltpu.CompilerParams(vmem_limit_bytes=VMEM_LIMIT),
        cost_estimate=LIGHT,
    )(rows, rows, gu)


def down_kernel(slots, hidden_b_ref, hidden_c_ref, dn_ref, dn_second_ref, out_ref):
    step = dn_ref.shape[1]
    hidden_c = hidden_c_ref[...]
    row = lax.broadcasted_iota(jnp.int32, (hidden_c.shape[0], step), 0)
    out_ref[:, :step] = dot(hidden_b_ref[...], dn_ref[...]).astype(BF16)
    out_ref[:, step : 2 * step] = dot(hidden_b_ref[...], dn_second_ref[...]).astype(BF16)
    first, second = dot(hidden_c, dn_ref[...]), dot(hidden_c, dn_second_ref[...])
    folded = jnp.where(row % slots < slots // 2, first, second)
    out_ref[:, 2 * step :] = folded.astype(BF16)


def down_projection(slots, hidden_b, hidden_c, dn):
    n, hid = hidden_b.shape
    width = dn.shape[1]
    step = width // 8
    return pl.pallas_call(
        functools.partial(down_kernel, slots),
        out_shape=jax.ShapeDtypeStruct((n, 12 * step), BF16),
        grid=(4,),
        in_specs=[
            pl.BlockSpec((n, hid), lambda k: (0, 0)),
            pl.BlockSpec((n, hid), lambda k: (0, 0)),
            pl.BlockSpec((hid, step), lambda k: (0, k)),
            pl.BlockSpec((hid, step), lambda k: (0, 4 + k)),
        ],
        out_specs=pl.BlockSpec((n, 3 * step), lambda k: (0, k)),
        compiler_params=pltpu.CompilerParams(vmem_limit_bytes=VMEM_LIMIT),
        cost_estimate=LIGHT,
    )(hidden_b, hidden_c, dn, dn)


def mix_kernel(share_b_ref, share_c_ref, rows_ref, folded_ref, out_ref):
    n = out_ref.shape[1]
    both = dot(share_b_ref[...], rows_ref[...]) + dot(share_c_ref[...], folded_ref[...])
    out_ref[0] = (both[:n] + both[n:]).astype(BF16)


def mix_whole(share_b, share_c, rows):
    n = rows.shape[0]
    width = rows.shape[1] * 2 // 3
    two = share_b.shape[0]
    step = width // 8
    return pl.pallas_call(
        mix_kernel,
        out_shape=jax.ShapeDtypeStruct((4, two // 2, width // 4), BF16),
        grid=(8,),
        in_specs=[
            pl.BlockSpec((two, n), lambda k: (0, 0)),
            pl.BlockSpec((two, n), lambda k: (k // 4, 0)),
            pl.BlockSpec((n, step), lambda k: (0, 3 * (k % 4) + k // 4)),
            pl.BlockSpec((n, step), lambda k: (0, 3 * (k % 4) + 2)),
        ],
        out_specs=pl.BlockSpec((1, two // 2, step), lambda k: (k // 2, 0, k % 2)),
        compiler_params=pltpu.CompilerParams(vmem_limit_bytes=VMEM_LIMIT),
        cost_estimate=LIGHT,
    )(share_b, share_c, rows, rows)


def shards(
    tokens,
    routes,
    route_weight,
    gate_weight,
    up_weight,
    down_weight,
    delta_values,
    delta_owner,
    delta_index,
    delta_scale,
    delta_count,
):
    n_expert = lax.axis_size("expert")
    n_group = lax.axis_size("group")
    sources = n_expert * n_group
    me = lax.axis_index("group")
    tok_rows, quarter = tokens.shape
    width, hid = gate_weight.shape[1:]
    listed = delta_owner.shape[1]
    top_count = routes.shape[1]
    capacity = tok_rows * top_count * 9 // (8 * n_expert)
    slots_a = SLOTS_A
    slots_b, slots_c = SLOTS_B, SLOTS_C
    assert slots_a + slots_b + slots_c == capacity and slots_b == 2 * slots_c
    half = width // 2
    gate, up, down = gate_weight[0], up_weight[0], down_weight[0]

    def shift(x, by):
        return lax.ppermute(x, "group", ring(n_group, by))

    def exchange(x, axes):
        return lax.all_to_all(x, axes, split_axis=0, concat_axis=0, tiled=True)

    order = jnp.stack([me, (me + 3) % 4, (me + 1) % 4, (me + 2) % 4]).astype(jnp.int32)

    named = routes[:, :, None] == jnp.arange(n_expert, dtype=jnp.int32)
    member = jnp.any(named, axis=1)
    share = jnp.sum(jnp.where(named, route_weight[:, :, None], 0.0), axis=1)
    before = jnp.tri(tok_rows, k=-1, dtype=BF16)
    rank = dot(before, member.astype(BF16)).astype(jnp.int32)
    rank = jnp.where(member, rank, -1).T
    slot_a = jnp.arange(slots_a, dtype=jnp.int32)
    slot_b = jnp.arange(slots_a, slots_a + slots_b, dtype=jnp.int32)
    slot_c = slots_a + slots_b + slot_b % slots_c
    front = (slot_b - slots_a) < slots_c
    slot_c0, slot_c1 = jnp.where(front, slot_c, -2), jnp.where(front, -2, slot_c)

    def pick(slots):
        hit = rank[:, None, :] == slots[None, :, None]
        return hit.astype(BF16).reshape(n_expert * slots.shape[0], tok_rows)

    def shares(slots):
        hit = rank.T[:, :, None] == slots[None, None, :]
        table = jnp.where(hit, share[:, :, None], 0.0)
        return two_parts(table.reshape(tok_rows, n_expert * slots.shape[0]))

    pick_a = lax.optimization_barrier(pick(slot_a))

    send_a = dot(pick_a, tokens).astype(BF16)
    send_a, tokens = lax.optimization_barrier((send_a, tokens))
    tokens_all = jnp.concatenate(
        [tokens, shift(tokens, 1), shift(tokens, -1), shift(tokens, 2)], axis=1
    )
    recv_a = exchange(send_a.reshape(n_expert, slots_a, quarter), "expert")
    rows_a = recv_a.reshape(n_expert * slots_a, quarter)

    live = jnp.arange(listed, dtype=jnp.int32) < delta_count[0]
    to = (delta_owner[0][None, :] == jnp.arange(sources, dtype=jnp.int32)[:, None]) & live[None, :]
    slot_out = jnp.sum(jnp.where(to, delta_index[0][None, :] + 1, 0), axis=1)
    scale_out = jnp.sum(jnp.where(to, delta_scale[0][None, :], 0), axis=1)
    meta = jnp.stack([slot_out // 8, slot_out % 8, scale_out], axis=1)
    meta = jnp.pad(meta, ((0, 0), (0, META - 3))).astype(BF16)
    meta = jnp.broadcast_to(meta[:, :, None], (sources, META, BLOCK))
    blocks = delta_values.reshape(listed, BLOCK, BLOCK)
    blocks, meta, tokens_all = lax.optimization_barrier((blocks, meta, tokens_all))
    outgoing = spread_blocks(delta_owner[0], delta_count, blocks, meta)
    incoming = exchange(outgoing, ("expert", "group"))

    gu, dn = arrange(order, gate, up, down)

    pick_c = jnp.concatenate([pick(slot_c0), pick(slot_c1)], axis=1)
    share_c = jnp.concatenate([shares(slot_c0), shares(slot_c1)], axis=0)
    tables = (pick(slot_b), pick_c, shares(slot_a), shares(slot_b), share_c)
    pick_b, pick_c, share_a, share_b, share_c = lax.optimization_barrier(tables)
    tokens_all, gu, dn = lax.optimization_barrier((tokens_all, gu, dn))
    send_b = dot(pick_b, tokens_all).astype(BF16)
    halves = jnp.concatenate([tokens_all[:, :half], tokens_all[:, half:]], axis=0)
    send_c = dot(pick_c, halves).astype(BF16)
    send_b = jnp.concatenate([send_b, send_c], axis=1)

    rows = n_expert * slots_a // 2
    after, ahead = shift(rows_a, 1), shift(rows_a, -1)
    far_top, far_bottom = shift(after[:rows], 1), shift(ahead[rows:], -1)

    send_b, incoming = lax.optimization_barrier((send_b, incoming))
    recv_b = exchange(send_b.reshape(n_expert, slots_b, width + half), "expert")
    rows_b = recv_b.reshape(n_expert * slots_b, width + half)

    meta_in = incoming[:, BLOCK : BLOCK + META, 0].astype(jnp.int32)
    slot = meta_in[:, 0] * 8 + meta_in[:, 1] - 1
    scale = jnp.exp2(meta_in[:, 2].astype(F32))
    same = slot[:, None] == slot[None, :]
    entry = jnp.arange(sources, dtype=jnp.int32)
    first = jnp.min(jnp.where(same, entry[None, :], sources), axis=1)
    first = jnp.where(slot >= 0, first, -1)
    row_blocks, col_blocks = width // BLOCK, hid // BLOCK
    per_matrix = row_blocks * col_blocks
    near = row_blocks // n_group
    slot = jnp.maximum(slot, 0)
    matrix = slot // per_matrix
    inside = slot % per_matrix
    is_down = matrix == 2
    wide = jnp.where(is_down, inside % row_blocks, inside // col_blocks)
    narrow = jnp.where(is_down, inside // row_blocks, inside % col_blocks)
    distance = (wide // near - me + n_group) % n_group
    place = jnp.where(distance == 0, 0, jnp.where(distance == 3, 1, distance + 1))
    moved = place * near + wide % near
    where = jnp.stack(
        [
            first,
            jnp.where(is_down, narrow, wide),
            jnp.where(is_down, wide, narrow),
            jnp.where(is_down, narrow, moved),
            jnp.where(is_down, moved, narrow + col_blocks * (matrix == 1)),
            matrix,
        ]
    ).astype(jnp.int32)
    factors = (width**-0.5, (hid * n_group) ** -0.5)
    gu, dn = patch(factors, where, scale, incoming, gate, up, down, gu, dn)

    acc = dot(rows_a, gu[:quarter])
    acc = acc + dot(after, gu[quarter : 2 * quarter])
    acc = acc + dot(ahead, gu[2 * quarter : 3 * quarter])
    acc, far_top, far_bottom = lax.optimization_barrier((acc, far_top, far_bottom))
    last = gu[3 * quarter :]
    hidden_top = silu_product(acc[:rows] + dot(far_top, last))
    hidden_bottom = silu_product(acc[rows:] + dot(far_bottom, last))

    def part(hidden, index):
        return dot(hidden, dn[:, index * quarter : (index + 1) * quarter])

    top_3, bottom_3 = part(hidden_top, 3).astype(BF16), part(hidden_bottom, 3).astype(BF16)
    top_3, bottom_3, rows_b = lax.optimization_barrier((top_3, bottom_3, rows_b))
    top_3, bottom_3 = shift(top_3, -1), shift(bottom_3, 1)

    hidden_b, hidden_c = up_projection(slots_b, rows_b, gu)
    part_b = down_projection(slots_b, hidden_b, hidden_c, dn)
    back_b = exchange(part_b.reshape(n_expert, slots_b, width + half), "expert")

    hidden_a = jnp.concatenate([hidden_top, hidden_bottom], axis=0)
    part_1, part_2 = part(hidden_a, 1), part(hidden_a, 2)
    none = jnp.zeros_like(top_3)
    part_1 = (part_1 + jnp.concatenate([top_3, none], axis=0).astype(F32)).astype(BF16)
    part_2 = (part_2 + jnp.concatenate([none, bottom_3], axis=0).astype(F32)).astype(BF16)
    part_1, part_2 = shift(part_1, -1), shift(part_2, 1)
    out_a = part(hidden_a, 0) + part_1.astype(F32) + part_2.astype(F32)
    out_a, back_b = lax.optimization_barrier((out_a.astype(BF16), back_b))
    back_a = exchange(out_a.reshape(n_expert, slots_a, quarter), "expert")

    mix_b = mix_whole(share_b, share_c, back_b.reshape(n_expert * slots_b, width + half))
    result = mix_b[0].astype(F32)
    for i, by in ((1, -1), (2, 1), (3, 2)):
        result = result + shift(mix_b[i], by).astype(F32)
    mix_a = weighted(share_a, back_a.reshape(n_expert * slots_a, quarter))
    return (result + mix_a).astype(BF16)


def solution(mesh):
    return jax.shard_map(
        shards,
        mesh=mesh,
        in_specs=(
            P("expert", "group"),
            P("expert", None),
            P("expert", None),
            P("expert", None, "group"),
            P("expert", None, "group"),
            P("expert", "group", None),
            P(("expert", "group"), None),
            P(("expert", "group"), None),
            P(("expert", "group"), None),
            P(("expert", "group"), None),
            P(("expert", "group")),
        ),
        out_specs=P("expert", "group"),
        check_vma=False,
    )
```

```python
import functools

import jax
import jax.numpy as jnp
from jax import lax
from jax.experimental import pallas as pl
from jax.experimental.pallas import tpu as pltpu
from jax.sharding import PartitionSpec as P

BLOCK = 128
META = 8
SLOTS_A = 24
SLOTS_B = 8
SLOTS_C = 4
VMEM_LIMIT = 60 * 2**20
BF16 = jnp.bfloat16
F32 = jnp.float32
LIGHT = pl.CostEstimate(flops=0, bytes_accessed=0, transcendentals=0)
HBM = pl.BlockSpec(memory_space=pltpu.HBM)


def ring(n, shift):
    return [(i, (i + shift) % n) for i in range(n)]


def spread_kernel(owner_ref, count_ref, blocks_ref, meta_ref, out_ref):
    out_ref[:, BLOCK:, :] = meta_ref[...]

    def put(i, carry):
        out_ref[owner_ref[i], :BLOCK, :] = blocks_ref[i]
        return carry

    lax.fori_loop(0, count_ref[0], put, 0)


def spread_blocks(owner, count, blocks, meta):
    sources = meta.shape[0]
    shape = (sources, BLOCK + META, BLOCK)
    return pl.pallas_call(
        spread_kernel,
        out_shape=jax.ShapeDtypeStruct(shape, BF16),
        grid_spec=pltpu.PrefetchScalarGridSpec(
            num_scalar_prefetch=2,
            grid=(1,),
            in_specs=[
                pl.BlockSpec(blocks.shape, lambda i, *_: (0, 0, 0)),
                pl.BlockSpec(meta.shape, lambda i, *_: (0, 0, 0)),
            ],
            out_specs=pl.BlockSpec(shape, lambda i, *_: (0, 0, 0)),
        ),
        compiler_params=pltpu.CompilerParams(vmem_limit_bytes=VMEM_LIMIT),
        cost_estimate=LIGHT,
    )(owner, count, blocks, meta)


def arrange_kernel(order_ref, gate_ref, up_ref, down_ref, gu_ref, dn_ref):
    hid = gate_ref.shape[1]
    gu_ref[:, :hid] = gate_ref[...]
    gu_ref[:, hid:] = up_ref[...]
    dn_ref[...] = down_ref[...]


def arrange(order, gate, up, down):
    width, hid = gate.shape
    n = order.shape[0]
    parts = 2
    step = width // (n * parts)

    def rows(i, order_ref):
        return (order_ref[i // parts] * parts + i % parts, 0)

    def cols(i, order_ref):
        return (0, order_ref[i // parts] * parts + i % parts)

    return pl.pallas_call(
        arrange_kernel,
        out_shape=(
            jax.ShapeDtypeStruct((width, 2 * hid), BF16),
            jax.ShapeDtypeStruct((hid, width), BF16),
        ),
        grid_spec=pltpu.PrefetchScalarGridSpec(
            num_scalar_prefetch=1,
            grid=(n * parts,),
            in_specs=[
                pl.BlockSpec((step, hid), rows),
                pl.BlockSpec((step, hid), rows),
                pl.BlockSpec((hid, step), cols),
            ],
            out_specs=[
                pl.BlockSpec((step, 2 * hid), lambda i, order_ref: (i, 0)),
                pl.BlockSpec((hid, step), lambda i, order_ref: (0, i)),
            ],
        ),
        compiler_params=pltpu.CompilerParams(vmem_limit_bytes=VMEM_LIMIT),
        cost_estimate=LIGHT,
    )(order, gate, up, down)


def patch_kernel(
    factors,
    where_ref,
    scale_ref,
    incoming_ref,
    gate_ref,
    up_ref,
    down_ref,
    gu_in_ref,
    dn_in_ref,
    gu_ref,
    dn_ref,
    blocks,
    held,
    total,
    in_sems,
    out_sems,
    block_sem,
):
    sources = blocks.shape[0]
    load = pltpu.make_async_copy(
        incoming_ref.at[:, pl.ds(0, BLOCK), :], blocks, block_sem.at[0]
    )
    load.start()

    def block_of(ref, row, col):
        return ref.at[
            pl.ds(pl.multiple_of(row * BLOCK, BLOCK), BLOCK),
            pl.ds(pl.multiple_of(col * BLOCK, BLOCK), BLOCK),
        ]

    def fetch(s, ref):
        return pltpu.make_async_copy(
            block_of(ref, where_ref[1, s], where_ref[2, s]), held.at[s], in_sems.at[s]
        )

    def put(s, ref):
        return pltpu.make_async_copy(
            held.at[s], block_of(ref, where_ref[3, s], where_ref[4, s]), out_sems.at[s]
        )

    corner = gate_ref.at[pl.ds(0, BLOCK), pl.ds(0, BLOCK)]

    def arrived(s):
        return pltpu.make_async_copy(corner, held.at[s], in_sems.at[s])

    def written(s):
        return pltpu.make_async_copy(
            held.at[s], gu_ref.at[pl.ds(0, BLOCK), pl.ds(0, BLOCK)], out_sems.at[s]
        )

    def leads(s):
        return where_ref[0, s] == s

    def start(s, carry):
        for m, ref in enumerate((gate_ref, up_ref, down_ref)):

            @pl.when(leads(s) & (where_ref[5, s] == m))
            def _():
                fetch(s, ref).start()

        return carry

    lax.fori_loop(0, sources, start, 0)
    load.wait()

    def add(s, carry):
        first = where_ref[0, s]

        @pl.when(first == s)
        def _():
            total[s] = blocks[s].astype(F32) * scale_ref[s]

        @pl.when((first >= 0) & (first != s))
        def _():
            total[first] = total[first] + blocks[s].astype(F32) * scale_ref[s]

        return carry

    lax.fori_loop(0, sources, add, 0)

    def finish(s, carry):
        @pl.when(leads(s))
        def _():
            arrived(s).wait()
            factor = jnp.where(where_ref[5, s] == 2, F32(factors[1]), F32(factors[0]))
            held[s] = (held[s].astype(F32) + factor * total[s]).astype(BF16)

        @pl.when(leads(s) & (where_ref[5, s] < 2))
        def _():
            put(s, gu_ref).start()

        @pl.when(leads(s) & (where_ref[5, s] == 2))
        def _():
            put(s, dn_ref).start()

        return carry

    lax.fori_loop(0, sources, finish, 0)

    def drain(s, carry):
        @pl.when(leads(s))
        def _():
            written(s).wait()

        return carry

    lax.fori_loop(0, sources, drain, 0)


def patch(factors, where, scale, incoming, gate, up, down, gu, dn):
    sources = incoming.shape[0]
    return pl.pallas_call(
        functools.partial(patch_kernel, factors),
        out_shape=(
            jax.ShapeDtypeStruct(gu.shape, BF16),
            jax.ShapeDtypeStruct(dn.shape, BF16),
        ),
        grid_spec=pltpu.PrefetchScalarGridSpec(
            num_scalar_prefetch=2,
            grid=(1,),
            in_specs=[HBM] * 6,
            out_specs=[HBM, HBM],
            scratch_shapes=[
                pltpu.VMEM((sources, BLOCK, BLOCK), BF16),
                pltpu.VMEM((sources, BLOCK, BLOCK), BF16),
                pltpu.VMEM((sources, BLOCK, BLOCK), F32),
                pltpu.SemaphoreType.DMA((sources,)),
                pltpu.SemaphoreType.DMA((sources,)),
                pltpu.SemaphoreType.DMA((1,)),
            ],
        ),
        input_output_aliases={6: 0, 7: 1},
        compiler_params=pltpu.CompilerParams(vmem_limit_bytes=VMEM_LIMIT),
        cost_estimate=LIGHT,
    )(where, scale, incoming, gate, up, down, gu, dn)


def dot(a, b):
    return jnp.dot(a, b, preferred_element_type=F32)


def weighted(table, rows):
    both = dot(table, rows)
    n = both.shape[0] // 2
    return both[:n] + both[n:]


def two_parts(table):
    high = table.astype(BF16)
    low = (table - high.astype(F32)).astype(BF16)
    return jnp.concatenate([high, low], axis=0)


def silu_product(acc):
    hid = acc.shape[1] // 2
    return (jax.nn.silu(acc[:, :hid]) * acc[:, hid:]).astype(BF16)


def up_kernel(slots, rows_ref, folded_ref, gu_ref, hidden_b_ref, hidden_c_ref, acc, rows, pick):
    step, steps = pl.program_id(0), pl.num_programs(0)
    n = rows_ref.shape[0]

    @pl.when(step == 0)
    def _():
        acc[...] = jnp.zeros_like(acc)

    @pl.when((step == 0) | (step == steps // 2))
    def _():
        row = lax.broadcasted_iota(jnp.int32, (n, n), 0)
        col = lax.broadcasted_iota(jnp.int32, (n, n), 1)
        same = (row // slots == col // slots) & (row % (slots // 2) == col % (slots // 2))
        second = (step >= steps // 2).astype(jnp.int32)
        here = same & ((col % slots) // (slots // 2) == second)
        pick[...] = jnp.where(here, 1.0, 0.0).astype(BF16)

    rows[:n] = rows_ref[...]
    rows[n:] = dot(pick[...], folded_ref[...]).astype(BF16)
    acc[...] += dot(rows[...], gu_ref[...])

    @pl.when(step == steps - 1)
    def _():
        hidden_b_ref[...] = silu_product(acc[:n])
        hidden_c_ref[...] = silu_product(acc[n:])


def up_projection(slots, rows, gu):
    n = rows.shape[0]
    width, wide = gu.shape
    steps = 4
    step = width // steps
    out = jax.ShapeDtypeStruct((n, wide // 2), BF16)
    return pl.pallas_call(
        functools.partial(up_kernel, slots),
        out_shape=(out, out),
        grid=(steps,),
        in_specs=[
            pl.BlockSpec((n, step), lambda k: (0, k)),
            pl.BlockSpec((n, step), lambda k: (0, steps + k % (steps // 2))),
            pl.BlockSpec((step, wide), lambda k: (k, 0)),
        ],
        out_specs=[pl.BlockSpec((n, wide // 2), lambda k: (0, 0))] * 2,
        scratch_shapes=[
            pltpu.VMEM((2 * n, wide), F32),
            pltpu.VMEM((2 * n, step), BF16),
            pltpu.VMEM((n, n), BF16),
        ],
        compiler_params=pltpu.CompilerParams(vmem_limit_bytes=VMEM_LIMIT),
        cost_estimate=LIGHT,
    )(rows, rows, gu)


def down_kernel(slots, hidden_b_ref, hidden_c_ref, dn_ref, dn_second_ref, out_ref):
    step = dn_ref.shape[1]
    hidden_c = hidden_c_ref[...]
    row = lax.broadcasted_iota(jnp.int32, (hidden_c.shape[0], step), 0)
    out_ref[:, :step] = dot(hidden_b_ref[...], dn_ref[...]).astype(BF16)
    out_ref[:, step : 2 * step] = dot(hidden_b_ref[...], dn_second_ref[...]).astype(BF16)
    first, second = dot(hidden_c, dn_ref[...]), dot(hidden_c, dn_second_ref[...])
    folded = jnp.where(row % slots < slots // 2, first, second)
    out_ref[:, 2 * step :] = folded.astype(BF16)


def down_projection(slots, hidden_b, hidden_c, dn):
    n, hid = hidden_b.shape
    width = dn.shape[1]
    step = width // 8
    return pl.pallas_call(
        functools.partial(down_kernel, slots),
        out_shape=jax.ShapeDtypeStruct((n, 12 * step), BF16),
        grid=(4,),
        in_specs=[
            pl.BlockSpec((n, hid), lambda k: (0, 0)),
            pl.BlockSpec((n, hid), lambda k: (0, 0)),
            pl.BlockSpec((hid, step), lambda k: (0, k)),
            pl.BlockSpec((hid, step), lambda k: (0, 4 + k)),
        ],
        out_specs=pl.BlockSpec((n, 3 * step), lambda k: (0, k)),
        compiler_params=pltpu.CompilerParams(vmem_limit_bytes=VMEM_LIMIT),
        cost_estimate=LIGHT,
    )(hidden_b, hidden_c, dn, dn)


def mix_kernel(share_b_ref, share_c_ref, rows_ref, folded_ref, out_ref):
    n = out_ref.shape[1]
    both = dot(share_b_ref[...], rows_ref[...]) + dot(share_c_ref[...], folded_ref[...])
    out_ref[0] = (both[:n] + both[n:]).astype(BF16)


def mix_whole(share_b, share_c, rows):
    n = rows.shape[0]
    width = rows.shape[1] * 2 // 3
    two = share_b.shape[0]
    step = width // 8
    return pl.pallas_call(
        mix_kernel,
        out_shape=jax.ShapeDtypeStruct((4, two // 2, width // 4), BF16),
        grid=(8,),
        in_specs=[
            pl.BlockSpec((two, n), lambda k: (0, 0)),
            pl.BlockSpec((two, n), lambda k: (k // 4, 0)),
            pl.BlockSpec((n, step), lambda k: (0, 3 * (k % 4) + k // 4)),
            pl.BlockSpec((n, step), lambda k: (0, 3 * (k % 4) + 2)),
        ],
        out_specs=pl.BlockSpec((1, two // 2, step), lambda k: (k // 2, 0, k % 2)),
        compiler_params=pltpu.CompilerParams(vmem_limit_bytes=VMEM_LIMIT),
        cost_estimate=LIGHT,
    )(share_b, share_c, rows, rows)


def shards(
    tokens,
    routes,
    route_weight,
    gate_weight,
    up_weight,
    down_weight,
    delta_values,
    delta_owner,
    delta_index,
    delta_scale,
    delta_count,
):
    n_expert = lax.axis_size("expert")
    n_group = lax.axis_size("group")
    sources = n_expert * n_group
    me = lax.axis_index("group")
    tok_rows, quarter = tokens.shape
    width, hid = gate_weight.shape[1:]
    listed = delta_owner.shape[1]
    top_count = routes.shape[1]
    capacity = tok_rows * top_count * 9 // (8 * n_expert)
    slots_a = SLOTS_A
    slots_b, slots_c = SLOTS_B, SLOTS_C
    assert slots_a + slots_b + slots_c == capacity and slots_b == 2 * slots_c
    half = width // 2
    gate, up, down = gate_weight[0], up_weight[0], down_weight[0]

    def shift(x, by):
        return lax.ppermute(x, "group", ring(n_group, by))

    def exchange(x, axes):
        return lax.all_to_all(x, axes, split_axis=0, concat_axis=0, tiled=True)

    order = jnp.stack([me, (me + 3) % 4, (me + 1) % 4, (me + 2) % 4]).astype(jnp.int32)

    named = routes[:, :, None] == jnp.arange(n_expert, dtype=jnp.int32)
    member = jnp.any(named, axis=1)
    share = jnp.sum(jnp.where(named, route_weight[:, :, None], 0.0), axis=1)
    before = jnp.tri(tok_rows, k=-1, dtype=BF16)
    rank = dot(before, member.astype(BF16)).astype(jnp.int32)
    rank = jnp.where(member, rank, -1).T
    slot_a = jnp.arange(slots_a, dtype=jnp.int32)
    slot_b = jnp.arange(slots_a, slots_a + slots_b, dtype=jnp.int32)
    slot_c = slots_a + slots_b + slot_b % slots_c
    front = (slot_b - slots_a) < slots_c
    slot_c0, slot_c1 = jnp.where(front, slot_c, -2), jnp.where(front, -2, slot_c)

    def pick(slots):
        hit = rank[:, None, :] == slots[None, :, None]
        return hit.astype(BF16).reshape(n_expert * slots.shape[0], tok_rows)

    def shares(slots):
        hit = rank.T[:, :, None] == slots[None, None, :]
        table = jnp.where(hit, share[:, :, None], 0.0)
        return two_parts(table.reshape(tok_rows, n_expert * slots.shape[0]))

    pick_a = lax.optimization_barrier(pick(slot_a))

    send_a = dot(pick_a, tokens).astype(BF16)
    recv_a = exchange(send_a.reshape(n_expert, slots_a, quarter), "expert")
    rows_a = recv_a.reshape(n_expert * slots_a, quarter)

    live = jnp.arange(listed, dtype=jnp.int32) < delta_count[0]
    to = (delta_owner[0][None, :] == jnp.arange(sources, dtype=jnp.int32)[:, None]) & live[None, :]
    slot_out = jnp.sum(jnp.where(to, delta_index[0][None, :] + 1, 0), axis=1)
    scale_out = jnp.sum(jnp.where(to, delta_scale[0][None, :], 0), axis=1)
    meta = jnp.stack([slot_out // 8, slot_out % 8, scale_out], axis=1)
    meta = jnp.pad(meta, ((0, 0), (0, META - 3))).astype(BF16)
    meta = jnp.broadcast_to(meta[:, :, None], (sources, META, BLOCK))
    blocks = delta_values.reshape(listed, BLOCK, BLOCK)
    blocks, meta, _ = lax.optimization_barrier((blocks, meta, send_a))
    outgoing = spread_blocks(delta_owner[0], delta_count, blocks, meta)
    tokens, outgoing = lax.optimization_barrier((tokens, outgoing))
    tokens_all = jnp.concatenate(
        [tokens, shift(tokens, 1), shift(tokens, -1), shift(tokens, 2)], axis=1
    )
    outgoing, _ = lax.optimization_barrier((outgoing, rows_a))
    incoming = exchange(outgoing, ("expert", "group"))

    gu, dn = arrange(order, gate, up, down)

    pick_c = jnp.concatenate([pick(slot_c0), pick(slot_c1)], axis=1)
    share_c = jnp.concatenate([shares(slot_c0), shares(slot_c1)], axis=0)
    tables = (pick(slot_b), pick_c, shares(slot_a), shares(slot_b), share_c)
    pick_b, pick_c, share_a, share_b, share_c = lax.optimization_barrier(tables)
    tokens_all, gu, dn = lax.optimization_barrier((tokens_all, gu, dn))
    send_b = dot(pick_b, tokens_all).astype(BF16)
    halves = jnp.concatenate([tokens_all[:, :half], tokens_all[:, half:]], axis=0)
    send_c = dot(pick_c, halves).astype(BF16)
    send_b = jnp.concatenate([send_b, send_c], axis=1)

    rows = n_expert * slots_a // 2
    top, bottom = rows_a[:rows], rows_a[rows:]
    after_top, ahead_bottom = shift(top, 1), shift(bottom, -1)
    after_bottom, ahead_top = shift(bottom, 1), shift(top, -1)

    send_b, incoming = lax.optimization_barrier((send_b, incoming))
    recv_b = exchange(send_b.reshape(n_expert, slots_b, width + half), "expert")
    rows_b = recv_b.reshape(n_expert * slots_b, width + half)

    meta_in = incoming[:, BLOCK : BLOCK + META, 0].astype(jnp.int32)
    slot = meta_in[:, 0] * 8 + meta_in[:, 1] - 1
    scale = jnp.exp2(meta_in[:, 2].astype(F32))
    same = slot[:, None] == slot[None, :]
    entry = jnp.arange(sources, dtype=jnp.int32)
    first = jnp.min(jnp.where(same, entry[None, :], sources), axis=1)
    first = jnp.where(slot >= 0, first, -1)
    row_blocks, col_blocks = width // BLOCK, hid // BLOCK
    per_matrix = row_blocks * col_blocks
    near = row_blocks // n_group
    slot = jnp.maximum(slot, 0)
    matrix = slot // per_matrix
    inside = slot % per_matrix
    is_down = matrix == 2
    wide = jnp.where(is_down, inside % row_blocks, inside // col_blocks)
    narrow = jnp.where(is_down, inside // row_blocks, inside % col_blocks)
    distance = (wide // near - me + n_group) % n_group
    place = jnp.where(distance == 0, 0, jnp.where(distance == 3, 1, distance + 1))
    moved = place * near + wide % near
    where = jnp.stack(
        [
            first,
            jnp.where(is_down, narrow, wide),
            jnp.where(is_down, wide, narrow),
            jnp.where(is_down, narrow, moved),
            jnp.where(is_down, moved, narrow + col_blocks * (matrix == 1)),
            matrix,
        ]
    ).astype(jnp.int32)
    factors = (width**-0.5, (hid * n_group) ** -0.5)
    gu, dn = patch(factors, where, scale, incoming, gate, up, down, gu, dn)

    gu, after_top, ahead_bottom = lax.optimization_barrier((gu, after_top, ahead_bottom))
    far_top, far_bottom = shift(after_top, 1), shift(ahead_bottom, -1)
    acc = dot(rows_a, gu[:quarter])

    def near_products(acc, after, ahead):
        acc = acc + dot(after, gu[quarter : 2 * quarter])
        return acc + dot(ahead, gu[2 * quarter : 3 * quarter])

    acc_top = near_products(acc[:rows], after_top, ahead_top)
    acc_bottom = near_products(acc[rows:], after_bottom, ahead_bottom)
    acc_top, acc_bottom, far_top, far_bottom = lax.optimization_barrier(
        (acc_top, acc_bottom, far_top, far_bottom)
    )
    last = gu[3 * quarter :]
    hidden_top = silu_product(acc_top + dot(far_top, last))
    hidden_bottom = silu_product(acc_bottom + dot(far_bottom, last))

    def part(hidden, index):
        return dot(hidden, dn[:, index * quarter : (index + 1) * quarter])

    top_3, bottom_3 = part(hidden_top, 3).astype(BF16), part(hidden_bottom, 3).astype(BF16)
    top_3, bottom_3, rows_b = lax.optimization_barrier((top_3, bottom_3, rows_b))
    top_3, bottom_3 = shift(top_3, -1), shift(bottom_3, 1)

    hidden_b, hidden_c = up_projection(slots_b, rows_b, gu)
    part_b = down_projection(slots_b, hidden_b, hidden_c, dn)
    back_b = exchange(part_b.reshape(n_expert, slots_b, width + half), "expert")

    hidden_a = jnp.concatenate([hidden_top, hidden_bottom], axis=0)
    part_1, part_2 = part(hidden_a, 1), part(hidden_a, 2)
    none = jnp.zeros_like(top_3)
    part_1 = (part_1 + jnp.concatenate([top_3, none], axis=0).astype(F32)).astype(BF16)
    part_2 = (part_2 + jnp.concatenate([none, bottom_3], axis=0).astype(F32)).astype(BF16)
    part_1, part_2 = lax.optimization_barrier((part_1, part_2))
    part_1, part_2 = shift(part_1, -1), shift(part_2, 1)
    out_a = part(hidden_a, 0) + part_1.astype(F32) + part_2.astype(F32)
    out_a, back_b = lax.optimization_barrier((out_a.astype(BF16), back_b))
    back_a = exchange(out_a.reshape(n_expert, slots_a, quarter), "expert")

    mix_b = mix_whole(share_b, share_c, back_b.reshape(n_expert * slots_b, width + half))
    result = mix_b[0].astype(F32)
    for i, by in ((1, -1), (2, 1), (3, 2)):
        result = result + shift(mix_b[i], by).astype(F32)
    mix_a = weighted(share_a, back_a.reshape(n_expert * slots_a, quarter))
    return (result + mix_a).astype(BF16)


def solution(mesh):
    return jax.shard_map(
        shards,
        mesh=mesh,
        in_specs=(
            P("expert", "group"),
            P("expert", None),
            P("expert", None),
            P("expert", None, "group"),
            P("expert", None, "group"),
            P("expert", "group", None),
            P(("expert", "group"), None),
            P(("expert", "group"), None),
            P(("expert", "group"), None),
            P(("expert", "group"), None),
            P(("expert", "group")),
        ),
        out_specs=P("expert", "group"),
        check_vma=False,
    )
```

```python
import functools

import jax
import jax.numpy as jnp
from jax import lax
from jax.experimental import pallas as pl
from jax.experimental.pallas import tpu as pltpu
from jax.sharding import PartitionSpec as P

BLOCK = 128
META = 8
SLOTS_A = 24
SLOTS_B = 8
SLOTS_C = 4
VMEM_LIMIT = 60 * 2**20
BF16 = jnp.bfloat16
F32 = jnp.float32
LIGHT = pl.CostEstimate(flops=0, bytes_accessed=0, transcendentals=0)
HBM = pl.BlockSpec(memory_space=pltpu.HBM)


def ring(n, shift):
    return [(i, (i + shift) % n) for i in range(n)]


def spread_kernel(owner_ref, count_ref, blocks_ref, meta_ref, out_ref):
    out_ref[:, BLOCK:, :] = meta_ref[...]

    def put(i, carry):
        out_ref[owner_ref[i], :BLOCK, :] = blocks_ref[i]
        return carry

    lax.fori_loop(0, count_ref[0], put, 0)


def spread_blocks(owner, count, blocks, meta):
    sources = meta.shape[0]
    shape = (sources, BLOCK + META, BLOCK)
    return pl.pallas_call(
        spread_kernel,
        out_shape=jax.ShapeDtypeStruct(shape, BF16),
        grid_spec=pltpu.PrefetchScalarGridSpec(
            num_scalar_prefetch=2,
            grid=(1,),
            in_specs=[
                pl.BlockSpec(blocks.shape, lambda i, *_: (0, 0, 0)),
                pl.BlockSpec(meta.shape, lambda i, *_: (0, 0, 0)),
            ],
            out_specs=pl.BlockSpec(shape, lambda i, *_: (0, 0, 0)),
        ),
        compiler_params=pltpu.CompilerParams(vmem_limit_bytes=VMEM_LIMIT),
        cost_estimate=LIGHT,
    )(owner, count, blocks, meta)


def arrange_kernel(order_ref, gate_ref, up_ref, down_ref, gu_ref, dn_ref):
    hid = gate_ref.shape[1]
    gu_ref[:, :hid] = gate_ref[...]
    gu_ref[:, hid:] = up_ref[...]
    dn_ref[...] = down_ref[...]


def arrange(order, gate, up, down):
    width, hid = gate.shape
    n = order.shape[0]
    parts = 2
    step = width // (n * parts)

    def rows(i, order_ref):
        return (order_ref[i // parts] * parts + i % parts, 0)

    def cols(i, order_ref):
        return (0, order_ref[i // parts] * parts + i % parts)

    return pl.pallas_call(
        arrange_kernel,
        out_shape=(
            jax.ShapeDtypeStruct((width, 2 * hid), BF16),
            jax.ShapeDtypeStruct((hid, width), BF16),
        ),
        grid_spec=pltpu.PrefetchScalarGridSpec(
            num_scalar_prefetch=1,
            grid=(n * parts,),
            in_specs=[
                pl.BlockSpec((step, hid), rows),
                pl.BlockSpec((step, hid), rows),
                pl.BlockSpec((hid, step), cols),
            ],
            out_specs=[
                pl.BlockSpec((step, 2 * hid), lambda i, order_ref: (i, 0)),
                pl.BlockSpec((hid, step), lambda i, order_ref: (0, i)),
            ],
        ),
        compiler_params=pltpu.CompilerParams(vmem_limit_bytes=VMEM_LIMIT),
        cost_estimate=LIGHT,
    )(order, gate, up, down)


def patch_kernel(
    factors,
    where_ref,
    scale_ref,
    incoming_ref,
    gate_ref,
    up_ref,
    down_ref,
    gu_in_ref,
    dn_in_ref,
    gu_ref,
    dn_ref,
    blocks,
    held,
    total,
    in_sems,
    out_sems,
    block_sem,
):
    sources = blocks.shape[0]
    load = pltpu.make_async_copy(
        incoming_ref.at[:, pl.ds(0, BLOCK), :], blocks, block_sem.at[0]
    )
    load.start()

    def block_of(ref, row, col):
        return ref.at[
            pl.ds(pl.multiple_of(row * BLOCK, BLOCK), BLOCK),
            pl.ds(pl.multiple_of(col * BLOCK, BLOCK), BLOCK),
        ]

    def fetch(s, ref):
        return pltpu.make_async_copy(
            block_of(ref, where_ref[1, s], where_ref[2, s]), held.at[s], in_sems.at[s]
        )

    def put(s, ref):
        return pltpu.make_async_copy(
            held.at[s], block_of(ref, where_ref[3, s], where_ref[4, s]), out_sems.at[s]
        )

    corner = gate_ref.at[pl.ds(0, BLOCK), pl.ds(0, BLOCK)]

    def arrived(s):
        return pltpu.make_async_copy(corner, held.at[s], in_sems.at[s])

    def written(s):
        return pltpu.make_async_copy(
            held.at[s], gu_ref.at[pl.ds(0, BLOCK), pl.ds(0, BLOCK)], out_sems.at[s]
        )

    def leads(s):
        return where_ref[0, s] == s

    def start(s, carry):
        for m, ref in enumerate((gate_ref, up_ref, down_ref)):

            @pl.when(leads(s) & (where_ref[5, s] == m))
            def _():
                fetch(s, ref).start()

        return carry

    lax.fori_loop(0, sources, start, 0)
    load.wait()

    def add(s, carry):
        first = where_ref[0, s]

        @pl.when(first == s)
        def _():
            total[s] = blocks[s].astype(F32) * scale_ref[s]

        @pl.when((first >= 0) & (first != s))
        def _():
            total[first] = total[first] + blocks[s].astype(F32) * scale_ref[s]

        return carry

    lax.fori_loop(0, sources, add, 0)

    def finish(s, carry):
        @pl.when(leads(s))
        def _():
            arrived(s).wait()
            factor = jnp.where(where_ref[5, s] == 2, F32(factors[1]), F32(factors[0]))
            held[s] = (held[s].astype(F32) + factor * total[s]).astype(BF16)

        @pl.when(leads(s) & (where_ref[5, s] < 2))
        def _():
            put(s, gu_ref).start()

        @pl.when(leads(s) & (where_ref[5, s] == 2))
        def _():
            put(s, dn_ref).start()

        return carry

    lax.fori_loop(0, sources, finish, 0)

    def drain(s, carry):
        @pl.when(leads(s))
        def _():
            written(s).wait()

        return carry

    lax.fori_loop(0, sources, drain, 0)


def patch(factors, where, scale, incoming, gate, up, down, gu, dn):
    sources = incoming.shape[0]
    return pl.pallas_call(
        functools.partial(patch_kernel, factors),
        out_shape=(
            jax.ShapeDtypeStruct(gu.shape, BF16),
            jax.ShapeDtypeStruct(dn.shape, BF16),
        ),
        grid_spec=pltpu.PrefetchScalarGridSpec(
            num_scalar_prefetch=2,
            grid=(1,),
            in_specs=[HBM] * 6,
            out_specs=[HBM, HBM],
            scratch_shapes=[
                pltpu.VMEM((sources, BLOCK, BLOCK), BF16),
                pltpu.VMEM((sources, BLOCK, BLOCK), BF16),
                pltpu.VMEM((sources, BLOCK, BLOCK), F32),
                pltpu.SemaphoreType.DMA((sources,)),
                pltpu.SemaphoreType.DMA((sources,)),
                pltpu.SemaphoreType.DMA((1,)),
            ],
        ),
        input_output_aliases={6: 0, 7: 1},
        compiler_params=pltpu.CompilerParams(vmem_limit_bytes=VMEM_LIMIT),
        cost_estimate=LIGHT,
    )(where, scale, incoming, gate, up, down, gu, dn)


def dot(a, b):
    return jnp.dot(a, b, preferred_element_type=F32)


def weighted(table, rows):
    both = dot(table, rows)
    n = both.shape[0] // 2
    return both[:n] + both[n:]


def two_parts(table):
    high = table.astype(BF16)
    low = (table - high.astype(F32)).astype(BF16)
    return jnp.concatenate([high, low], axis=0)


def silu_product(acc):
    hid = acc.shape[1] // 2
    return (jax.nn.silu(acc[:, :hid]) * acc[:, hid:]).astype(BF16)


def up_kernel(slots, rows_ref, folded_ref, gu_ref, hidden_b_ref, hidden_c_ref, acc, rows, pick):
    step, steps = pl.program_id(0), pl.num_programs(0)
    n = rows_ref.shape[0]

    @pl.when(step == 0)
    def _():
        acc[...] = jnp.zeros_like(acc)

    @pl.when((step == 0) | (step == steps // 2))
    def _():
        row = lax.broadcasted_iota(jnp.int32, (n, n), 0)
        col = lax.broadcasted_iota(jnp.int32, (n, n), 1)
        same = (row // slots == col // slots) & (row % (slots // 2) == col % (slots // 2))
        second = (step >= steps // 2).astype(jnp.int32)
        here = same & ((col % slots) // (slots // 2) == second)
        pick[...] = jnp.where(here, 1.0, 0.0).astype(BF16)

    rows[:n] = rows_ref[...]
    rows[n:] = dot(pick[...], folded_ref[...]).astype(BF16)
    acc[...] += dot(rows[...], gu_ref[...])

    @pl.when(step == steps - 1)
    def _():
        hidden_b_ref[...] = silu_product(acc[:n])
        hidden_c_ref[...] = silu_product(acc[n:])


def up_projection(slots, rows, gu):
    n = rows.shape[0]
    width, wide = gu.shape
    steps = 4
    step = width // steps
    out = jax.ShapeDtypeStruct((n, wide // 2), BF16)
    return pl.pallas_call(
        functools.partial(up_kernel, slots),
        out_shape=(out, out),
        grid=(steps,),
        in_specs=[
            pl.BlockSpec((n, step), lambda k: (0, k)),
            pl.BlockSpec((n, step), lambda k: (0, steps + k % (steps // 2))),
            pl.BlockSpec((step, wide), lambda k: (k, 0)),
        ],
        out_specs=[pl.BlockSpec((n, wide // 2), lambda k: (0, 0))] * 2,
        scratch_shapes=[
            pltpu.VMEM((2 * n, wide), F32),
            pltpu.VMEM((2 * n, step), BF16),
            pltpu.VMEM((n, n), BF16),
        ],
        compiler_params=pltpu.CompilerParams(vmem_limit_bytes=VMEM_LIMIT),
        cost_estimate=LIGHT,
    )(rows, rows, gu)


def down_kernel(slots, hidden_b_ref, hidden_c_ref, dn_ref, dn_second_ref, out_ref):
    step = dn_ref.shape[1]
    n = hidden_b_ref.shape[0]
    hidden = jnp.concatenate([hidden_b_ref[...], hidden_c_ref[...]], axis=0)
    first, second = dot(hidden, dn_ref[...]), dot(hidden, dn_second_ref[...])
    out_ref[:, :step] = first[:n].astype(BF16)
    out_ref[:, step : 2 * step] = second[:n].astype(BF16)
    row = lax.broadcasted_iota(jnp.int32, (n, step), 0)
    folded = jnp.where(row % slots < slots // 2, first[n:], second[n:])
    out_ref[:, 2 * step :] = folded.astype(BF16)


def down_projection(slots, hidden_b, hidden_c, dn):
    n, hid = hidden_b.shape
    width = dn.shape[1]
    step = width // 8
    return pl.pallas_call(
        functools.partial(down_kernel, slots),
        out_shape=jax.ShapeDtypeStruct((n, 12 * step), BF16),
        grid=(4,),
        in_specs=[
            pl.BlockSpec((n, hid), lambda k: (0, 0)),
            pl.BlockSpec((n, hid), lambda k: (0, 0)),
            pl.BlockSpec((hid, step), lambda k: (0, k)),
            pl.BlockSpec((hid, step), lambda k: (0, 4 + k)),
        ],
        out_specs=pl.BlockSpec((n, 3 * step), lambda k: (0, k)),
        compiler_params=pltpu.CompilerParams(vmem_limit_bytes=VMEM_LIMIT),
        cost_estimate=LIGHT,
    )(hidden_b, hidden_c, dn, dn)


def mix_kernel(share_b_ref, share_c_ref, rows_ref, folded_ref, out_ref):
    n = out_ref.shape[1]
    both = dot(share_b_ref[...], rows_ref[...]) + dot(share_c_ref[...], folded_ref[...])
    out_ref[0] = (both[:n] + both[n:]).astype(BF16)


def mix_whole(share_b, share_c, rows):
    n = rows.shape[0]
    width = rows.shape[1] * 2 // 3
    two = share_b.shape[0]
    step = width // 8
    return pl.pallas_call(
        mix_kernel,
        out_shape=jax.ShapeDtypeStruct((4, two // 2, width // 4), BF16),
        grid=(8,),
        in_specs=[
            pl.BlockSpec((two, n), lambda k: (0, 0)),
            pl.BlockSpec((two, n), lambda k: (k // 4, 0)),
            pl.BlockSpec((n, step), lambda k: (0, 3 * (k % 4) + k // 4)),
            pl.BlockSpec((n, step), lambda k: (0, 3 * (k % 4) + 2)),
        ],
        out_specs=pl.BlockSpec((1, two // 2, step), lambda k: (k // 2, 0, k % 2)),
        compiler_params=pltpu.CompilerParams(vmem_limit_bytes=VMEM_LIMIT),
        cost_estimate=LIGHT,
    )(share_b, share_c, rows, rows)


def shards(
    tokens,
    routes,
    route_weight,
    gate_weight,
    up_weight,
    down_weight,
    delta_values,
    delta_owner,
    delta_index,
    delta_scale,
    delta_count,
):
    n_expert = lax.axis_size("expert")
    n_group = lax.axis_size("group")
    sources = n_expert * n_group
    me = lax.axis_index("group")
    tok_rows, quarter = tokens.shape
    width, hid = gate_weight.shape[1:]
    listed = delta_owner.shape[1]
    top_count = routes.shape[1]
    capacity = tok_rows * top_count * 9 // (8 * n_expert)
    slots_a = SLOTS_A
    slots_b, slots_c = SLOTS_B, SLOTS_C
    assert slots_a + slots_b + slots_c == capacity and slots_b == 2 * slots_c
    half = width // 2
    gate, up, down = gate_weight[0], up_weight[0], down_weight[0]

    def shift(x, by):
        return lax.ppermute(x, "group", ring(n_group, by))

    def exchange(x, axes):
        return lax.all_to_all(x, axes, split_axis=0, concat_axis=0, tiled=True)

    order = jnp.stack([me, (me + 3) % 4, (me + 1) % 4, (me + 2) % 4]).astype(jnp.int32)

    named = routes[:, :, None] == jnp.arange(n_expert, dtype=jnp.int32)
    member = jnp.any(named, axis=1)
    share = jnp.sum(jnp.where(named, route_weight[:, :, None], 0.0), axis=1)
    before = jnp.tri(tok_rows, k=-1, dtype=BF16)
    rank = dot(before, member.astype(BF16)).astype(jnp.int32)
    rank = jnp.where(member, rank, -1).T
    slot_a = jnp.arange(slots_a, dtype=jnp.int32)
    slot_b = jnp.arange(slots_a, slots_a + slots_b, dtype=jnp.int32)
    slot_c = slots_a + slots_b + slot_b % slots_c
    front = (slot_b - slots_a) < slots_c
    slot_c0, slot_c1 = jnp.where(front, slot_c, -2), jnp.where(front, -2, slot_c)

    def pick(slots):
        hit = rank[:, None, :] == slots[None, :, None]
        return hit.astype(BF16).reshape(n_expert * slots.shape[0], tok_rows)

    def shares(slots):
        hit = rank.T[:, :, None] == slots[None, None, :]
        table = jnp.where(hit, share[:, :, None], 0.0)
        return two_parts(table.reshape(tok_rows, n_expert * slots.shape[0]))

    pick_a = lax.optimization_barrier(pick(slot_a))

    send_a = dot(pick_a, tokens).astype(BF16)
    recv_a = exchange(send_a.reshape(n_expert, slots_a, quarter), "expert")
    rows_a = recv_a.reshape(n_expert * slots_a, quarter)

    live = jnp.arange(listed, dtype=jnp.int32) < delta_count[0]
    to = (delta_owner[0][None, :] == jnp.arange(sources, dtype=jnp.int32)[:, None]) & live[None, :]
    slot_out = jnp.sum(jnp.where(to, delta_index[0][None, :] + 1, 0), axis=1)
    scale_out = jnp.sum(jnp.where(to, delta_scale[0][None, :], 0), axis=1)
    meta = jnp.stack([slot_out // 8, slot_out % 8, scale_out], axis=1)
    meta = jnp.pad(meta, ((0, 0), (0, META - 3))).astype(BF16)
    meta = jnp.broadcast_to(meta[:, :, None], (sources, META, BLOCK))
    blocks = delta_values.reshape(listed, BLOCK, BLOCK)
    blocks, meta, _ = lax.optimization_barrier((blocks, meta, send_a))
    outgoing = spread_blocks(delta_owner[0], delta_count, blocks, meta)
    tokens, outgoing = lax.optimization_barrier((tokens, outgoing))
    tokens_all = jnp.concatenate(
        [tokens, shift(tokens, 1), shift(tokens, -1), shift(tokens, 2)], axis=1
    )
    outgoing, _ = lax.optimization_barrier((outgoing, rows_a))
    incoming = exchange(outgoing, ("expert", "group"))

    gu, dn = arrange(order, gate, up, down)

    pick_c = jnp.concatenate([pick(slot_c0), pick(slot_c1)], axis=1)
    share_c = jnp.concatenate([shares(slot_c0), shares(slot_c1)], axis=0)
    tables = (pick(slot_b), pick_c, shares(slot_a), shares(slot_b), share_c)
    pick_b, pick_c, share_a, share_b, share_c = lax.optimization_barrier(tables)
    tokens_all, gu, dn = lax.optimization_barrier((tokens_all, gu, dn))
    send_b = dot(pick_b, tokens_all).astype(BF16)
    halves = jnp.concatenate([tokens_all[:, :half], tokens_all[:, half:]], axis=0)
    send_c = dot(pick_c, halves).astype(BF16)
    send_b = jnp.concatenate([send_b, send_c], axis=1)

    rows = n_expert * slots_a // 2
    top, bottom = rows_a[:rows], rows_a[rows:]
    after_top, ahead_bottom = shift(top, 1), shift(bottom, -1)
    after_bottom, ahead_top = shift(bottom, 1), shift(top, -1)

    send_b, incoming = lax.optimization_barrier((send_b, incoming))
    recv_b = exchange(send_b.reshape(n_expert, slots_b, width + half), "expert")
    rows_b = recv_b.reshape(n_expert * slots_b, width + half)

    meta_in = incoming[:, BLOCK : BLOCK + META, 0].astype(jnp.int32)
    slot = meta_in[:, 0] * 8 + meta_in[:, 1] - 1
    scale = jnp.exp2(meta_in[:, 2].astype(F32))
    same = slot[:, None] == slot[None, :]
    entry = jnp.arange(sources, dtype=jnp.int32)
    first = jnp.min(jnp.where(same, entry[None, :], sources), axis=1)
    first = jnp.where(slot >= 0, first, -1)
    row_blocks, col_blocks = width // BLOCK, hid // BLOCK
    per_matrix = row_blocks * col_blocks
    near = row_blocks // n_group
    slot = jnp.maximum(slot, 0)
    matrix = slot // per_matrix
    inside = slot % per_matrix
    is_down = matrix == 2
    wide = jnp.where(is_down, inside % row_blocks, inside // col_blocks)
    narrow = jnp.where(is_down, inside // row_blocks, inside % col_blocks)
    distance = (wide // near - me + n_group) % n_group
    place = jnp.where(distance == 0, 0, jnp.where(distance == 3, 1, distance + 1))
    moved = place * near + wide % near
    where = jnp.stack(
        [
            first,
            jnp.where(is_down, narrow, wide),
            jnp.where(is_down, wide, narrow),
            jnp.where(is_down, narrow, moved),
            jnp.where(is_down, moved, narrow + col_blocks * (matrix == 1)),
            matrix,
        ]
    ).astype(jnp.int32)
    factors = (width**-0.5, (hid * n_group) ** -0.5)
    gu, dn = patch(factors, where, scale, incoming, gate, up, down, gu, dn)

    gu, after_top, ahead_bottom = lax.optimization_barrier((gu, after_top, ahead_bottom))
    far_top, far_bottom = shift(after_top, 1), shift(ahead_bottom, -1)
    acc = dot(rows_a, gu[:quarter])

    def near_products(acc, after, ahead):
        acc = acc + dot(after, gu[quarter : 2 * quarter])
        return acc + dot(ahead, gu[2 * quarter : 3 * quarter])

    acc_top = near_products(acc[:rows], after_top, ahead_top)
    acc_bottom = near_products(acc[rows:], after_bottom, ahead_bottom)
    acc_top, acc_bottom, far_top, far_bottom = lax.optimization_barrier(
        (acc_top, acc_bottom, far_top, far_bottom)
    )
    last = gu[3 * quarter :]
    hidden_top = silu_product(acc_top + dot(far_top, last))
    hidden_bottom = silu_product(acc_bottom + dot(far_bottom, last))

    def part(hidden, index):
        return dot(hidden, dn[:, index * quarter : (index + 1) * quarter])

    top_3, bottom_3 = part(hidden_top, 3).astype(BF16), part(hidden_bottom, 3).astype(BF16)
    top_3, bottom_3, rows_b = lax.optimization_barrier((top_3, bottom_3, rows_b))
    top_3, bottom_3 = shift(top_3, -1), shift(bottom_3, 1)

    hidden_b, hidden_c = up_projection(slots_b, rows_b, gu)
    part_b = down_projection(slots_b, hidden_b, hidden_c, dn)
    back_b = exchange(part_b.reshape(n_expert, slots_b, width + half), "expert")

    hidden_a = jnp.concatenate([hidden_top, hidden_bottom], axis=0)
    part_1, part_2 = part(hidden_a, 1), part(hidden_a, 2)
    none = jnp.zeros_like(top_3)
    part_1 = (part_1 + jnp.concatenate([top_3, none], axis=0).astype(F32)).astype(BF16)
    part_2 = (part_2 + jnp.concatenate([none, bottom_3], axis=0).astype(F32)).astype(BF16)
    part_1, part_2 = lax.optimization_barrier((part_1, part_2))
    part_1, part_2 = shift(part_1, -1), shift(part_2, 1)
    out_a = part(hidden_a, 0) + part_1.astype(F32) + part_2.astype(F32)
    out_a, back_b = lax.optimization_barrier((out_a.astype(BF16), back_b))
    back_a = exchange(out_a.reshape(n_expert, slots_a, quarter), "expert")

    mix_b = mix_whole(share_b, share_c, back_b.reshape(n_expert * slots_b, width + half))
    result = mix_b[0].astype(F32)
    for i, by in ((1, -1), (2, 1), (3, 2)):
        result = result + shift(mix_b[i], by).astype(F32)
    mix_a = weighted(share_a, back_a.reshape(n_expert * slots_a, quarter))
    return (result + mix_a).astype(BF16)


def solution(mesh):
    return jax.shard_map(
        shards,
        mesh=mesh,
        in_specs=(
            P("expert", "group"),
            P("expert", None),
            P("expert", None),
            P("expert", None, "group"),
            P("expert", None, "group"),
            P("expert", "group", None),
            P(("expert", "group"), None),
            P(("expert", "group"), None),
            P(("expert", "group"), None),
            P(("expert", "group"), None),
            P(("expert", "group")),
        ),
        out_specs=P("expert", "group"),
        check_vma=False,
    )
```
